768 devices in a mesh: group: 24 (over z, core), expert: 32 (over y, x).
Axes of the slice: x: 4, y: 8, z: 12, core: 2. Of those that a mesh axis runs over, the one named last changes fastest.
Arguments:
- hidden_in: bfloat16 [98304, 1024], P(('group', 'expert')), parts along dimension 0, may hold values from -6 to 6
- out_grad: bfloat16 [98304, 1024], P(('group', 'expert')), parts along dimension 0, may hold values from -6 to 6
- gate_probs: float32 [98304, 2], P(('group', 'expert')), parts along dimension 0, may hold values from 0.25 to 2
- expert_ids: int32 [98304, 2], P(('group', 'expert')), parts along dimension 0, may hold values from 0 to 31, as said below
- w_gate: bfloat16 [32, 1024, 768], P('expert'), may hold values from -0.1875 to 0.1875
- w_up: bfloat16 [32, 1024, 768], P('expert'), may hold values from -0.1875 to 0.1875
- w_down: bfloat16 [32, 768, 1024], P('expert'), may hold values from -0.0546875 to 0.0546875
Outputs:
- input_grad: bfloat16 [98304, 1024], P(('group', 'expert')), parts along dimension 0
- prob_grad: bfloat16 [98304, 2], P(('group', 'expert')), parts along dimension 0
The draws below stay inside these ranges and needn't reach their ends.
There are 24 independent parts, one for each index of `group`. The reference program is written for one: setup_inputs(seed, part) draws one part's arguments, and reference() takes and returns one part's arrays. A program takes and returns all parts, laid end to end along the dimension named above; an argument that names none is the same for every part. Nothing has to cross between parts.
Inputs may be any that keep to these rules, and one draw needn't show every extreme that they name: `expert_ids`: each row names 2 different experts. Among the 128 rows of one device no expert is named more than 16 times, and in every draw one expert is named exactly 16 times by the rows of every device.
All inputs are finite; a program needn't handle non-finite values.
Results may differ from the reference program's by a relative error of at most 0.0057.
Values may be sent and summed in bfloat16 or wider, within the bound.
A program may use at most 32 MiB of HBM per device.

```python
import math
import jax
import jax.numpy as jnp
from jax import lax

D = 1024
FF = 768
EXPERTS = 32
TOPK = 2
TOK_DEV = 128
MOST = 16
TOKENS = 4096
N_EXPERT = 32


def draw_expert_ids(key, part):
    hot_key, rest_key = jax.random.split(jax.random.fold_in(key, 7))
    hot_expert = jax.random.randint(hot_key, (), 0, EXPERTS)
    expert_range = jnp.arange(EXPERTS, dtype=jnp.int32)
    offset = 1 << 28

    def one_block(block_key):
        order_key, noise_key = jax.random.split(block_key)
        order = jax.random.permutation(order_key, TOK_DEV)
        forced = order < MOST
        noise = jax.random.randint(noise_key, (TOK_DEV, EXPERTS), 0, 1 << 20)
        scores = noise * EXPERTS + expert_range[None, :]

        def choose(counts, inputs):
            row_scores, is_forced = inputs
            is_hot = expert_range == hot_expert
            blocked = jnp.logical_or(counts >= MOST, is_hot)
            picked = jnp.where(blocked, row_scores - offset, row_scores)
            picked = jnp.where(jnp.logical_and(is_hot, is_forced), row_scores + offset, picked)
            unused, chosen = lax.top_k(picked, TOPK)
            added = jnp.sum((chosen[:, None] == expert_range[None, :]).astype(jnp.int32), axis=0)
            return (counts + added, chosen.astype(jnp.int32))
        unused_counts, chosen_rows = lax.scan(choose, jnp.zeros((EXPERTS,), jnp.int32), (scores, forced))
        return chosen_rows
    block_keys = jax.random.split(rest_key, TOKENS // TOK_DEV)
    return jax.vmap(one_block)(block_keys).reshape(TOKENS, TOPK).astype(jnp.int32)


def level_of(key, dims, shards, low, high):
    gain, own = 1.0, jax.random.fold_in(key, 6)
    for axis_at, parts in shards:
        steps = jnp.exp(jax.random.uniform(jax.random.fold_in(own, axis_at), (parts,), jnp.float32, low / len(shards), high / len(shards)))
        gain = gain * jnp.repeat(steps, dims[axis_at] // parts).reshape([-1 if axis == axis_at else 1 for axis in range(len(dims))])
    return gain


def bell_draw(rng, dims, deviation, limit, cuts=(), kind=jnp.bfloat16):
    factor_of = level_of(rng, dims, cuts, -0.22, 0.18) if cuts else 1.0
    array = jax.random.normal(rng, dims, jnp.float32) * deviation * factor_of
    return jnp.minimum(jnp.maximum(array, -limit), limit).astype(kind)


def setup_inputs(seed: int = 0, part: int = 0) -> dict:
    keys = jax.random.split(jax.random.key(seed), 8)
    part_keys = jax.random.split(jax.random.fold_in(keys[7], part), 8)
    hidden_in = bell_draw(part_keys[0], (TOKENS, D), 1.0, 6.0, ((0, 32),))
    out_grad = bell_draw(part_keys[1], (TOKENS, D), 1.0, 6.0, ((0, 32),))
    gate_probs = jnp.clip(jnp.exp(math.log(2.0) - 2.0794415 * jax.random.uniform(part_keys[2], (TOKENS, TOPK), jnp.float32) ** level_of(part_keys[2], (TOKENS, TOPK), ((0, 32),), -0.2, 0.2)), 0.25, 2.0)
    expert_ids = draw_expert_ids(jax.random.fold_in(jax.random.fold_in(keys[7], part), 71), part)
    w_gate = bell_draw(keys[4], (EXPERTS, D, FF), D ** -0.5, 0.1875, ((0, 32),))
    w_up = bell_draw(keys[5], (EXPERTS, D, FF), D ** -0.5, 0.1875, ((0, 32),))
    w_down = bell_draw(keys[6], (EXPERTS, FF, D), (FF * D // 64) ** -0.5, 0.0546875, ((0, 32),))
    return {"hidden_in": hidden_in, "out_grad": out_grad, "gate_probs": gate_probs, "expert_ids": expert_ids, "w_gate": w_gate, "w_up": w_up, "w_down": w_down}


def expert_rows(rows_in, rows_grad, gate_w, up_w, down_w):
    gate_pre = jnp.dot(rows_in, gate_w, preferred_element_type=jnp.float32)
    up_pre = jnp.dot(rows_in, up_w, preferred_element_type=jnp.float32)
    sigmoid_a = jax.nn.sigmoid(gate_pre)
    silu_a = gate_pre * sigmoid_a
    hidden = silu_a * up_pre
    hidden_grad = jnp.dot(rows_grad, down_w.T, preferred_element_type=jnp.float32)
    prob_rows = jnp.sum(hidden_grad * hidden, axis=-1).astype(jnp.bfloat16)
    gate_grad = (hidden_grad * up_pre * sigmoid_a * (1.0 + gate_pre * (1.0 - sigmoid_a))).astype(jnp.bfloat16)
    up_grad = (hidden_grad * silu_a).astype(jnp.bfloat16)
    input_rows = jnp.dot(gate_grad, gate_w.T, preferred_element_type=jnp.float32)
    input_rows = input_rows + jnp.dot(up_grad, up_w.T, preferred_element_type=jnp.float32)
    return input_rows.astype(jnp.bfloat16), prob_rows


def reference(hidden_in, out_grad, gate_probs, expert_ids, w_gate, w_up, w_down):
    flat_ids = expert_ids.reshape(-1).astype(jnp.int32)
    total_rows = flat_ids.shape[0]
    capacity = N_EXPERT * MOST
    onehot = (flat_ids[:, None] == jnp.arange(EXPERTS, dtype=jnp.int32)[None, :]).astype(jnp.int32)
    slot_rank = jnp.sum((jnp.cumsum(onehot, axis=0) - 1) * onehot, axis=1).astype(jnp.int32)
    table = jnp.full((EXPERTS, capacity), total_rows, jnp.int32)
    table = table.at[flat_ids, slot_rank].set(jnp.arange(total_rows, dtype=jnp.int32))

    def per_expert(operands):
        gate_w, up_w, down_w, slot_rows = operands
        token_rows = (jnp.minimum(slot_rows, total_rows - 1) // TOPK).astype(jnp.int32)
        return expert_rows(hidden_in[token_rows], out_grad[token_rows], gate_w, up_w, down_w)

    input_rows, prob_rows = lax.map(per_expert, (w_gate, w_up, w_down, table))
    targets = table.reshape(-1)
    row_grads = jnp.zeros((total_rows, D), jnp.bfloat16).at[targets].set(input_rows.reshape(-1, D), mode="drop")
    prob_grads = jnp.zeros((total_rows,), jnp.bfloat16).at[targets].set(prob_rows.reshape(-1), mode="drop")
    weighted = row_grads.reshape(TOKENS, TOPK, D).astype(jnp.float32) * gate_probs[:, :, None]
    input_grad = jnp.sum(weighted, axis=1).astype(jnp.bfloat16)
    return input_grad, prob_grads.reshape(TOKENS, TOPK)
```

```python
import functools

import jax
import jax.numpy as jnp
from jax import lax
from jax.experimental import pallas as pl
from jax.experimental.pallas import tpu as pltpu
from jax.sharding import PartitionSpec as P

EXPERTS = 32
TOPK = 2
MOST = 16
NX = 4
NY = 8
CHUNKS = 4
PER = EXPERTS // CHUNKS
MESH = pl.DeviceIdType.MESH
BF16 = jnp.bfloat16
F32 = jnp.float32


def dot(a, b):
    return lax.dot_general(a, b, (((1,), (0,)), ((), ())), preferred_element_type=F32)


def dot_t(a, b):
    return lax.dot_general(a, b, (((1,), (1,)), ((), ())), preferred_element_type=F32)


def dy_of(c, half):
    if half == 0:
        return 4 - c
    return jnp.where(c == 0, 0, 4 + c)


def kernel(
    hid_ref, grad_ref, probs_ref, ids_ref, wg_hbm, wu_hbm, wd_hbm,
    out_ref, pg_ref,
    send_buf, recv_buf, back_send, back_recv, pb_send, pb_recv, wg, wu, wd,
    w_sem, fs_sem, fr_sem, bs_sem, br_sem, ps_sem, pr_sem,
):
    me = lax.axis_index("expert")
    my_y, my_x = me // NX, me % NX
    tok, width = hid_ref.shape
    ff = wg.shape[1]
    rows = PER * MOST

    barrier = pltpu.get_barrier_semaphore()

    def greet(i, carry):
        pl.semaphore_signal(barrier, inc=1, device_id={"expert": (me + i) % EXPERTS}, device_id_type=MESH)
        return carry

    lax.fori_loop(1, EXPERTS, greet, 0)
    weights = [
        pltpu.make_async_copy(wg_hbm.at[0], wg, w_sem.at[0]),
        pltpu.make_async_copy(wu_hbm.at[0], wu, w_sem.at[1]),
        pltpu.make_async_copy(wd_hbm.at[0], wd, w_sem.at[2]),
    ]
    for copy in weights:
        copy.start()

    ids = ids_ref[...]
    id0, id1 = ids[:, 0:1], ids[:, 1:2]
    lane = lax.broadcasted_iota(jnp.int32, (tok, tok), 1)
    sub = lax.broadcasted_iota(jnp.int32, (tok, tok), 0)
    named = jnp.logical_or(lane == id0, lane == id1)
    before = dot((lane < sub).astype(BF16), named.astype(BF16))
    rank0 = jnp.sum(jnp.where(lane == id0, before, 0.0), axis=1, keepdims=True).astype(jnp.int32)
    rank1 = jnp.sum(jnp.where(lane == id1, before, 0.0), axis=1, keepdims=True).astype(jnp.int32)
    tgt0, tgt1 = id0 * MOST + rank0, id1 * MOST + rank1
    eye = lane == sub
    row0 = jnp.sum(jnp.where(eye, tgt0, 0), axis=0, keepdims=True)
    row1 = jnp.sum(jnp.where(eye, tgt1, 0), axis=0, keepdims=True)
    half_rows = NX * MOST

    def pack(c):
        s = lax.broadcasted_iota(jnp.int32, (rows, tok), 0)
        y_a, y_b = (my_y + dy_of(c, 0)) % NY, (my_y + dy_of(c, 1)) % NY
        slot = jnp.where(s < half_rows, s + y_a * half_rows, s - half_rows + y_b * half_rows)
        pick = jnp.logical_or(slot == row0, slot == row1).astype(BF16)
        at = pl.ds(pl.multiple_of(c * rows, rows), rows)
        send_buf[at, :width] = dot(pick, hid_ref[...]).astype(BF16)
        send_buf[at, width:] = dot(pick, grad_ref[...]).astype(BF16)

    def out_copy(c, half, dx):
        i = c * 2 + half
        y = (my_y + dy_of(c, half)) % NY
        x = (my_x + dx) % NX
        slot = i * NX + my_x
        return pltpu.make_async_remote_copy(
            src_ref=send_buf.at[pl.ds(pl.multiple_of((i * NX + x) * MOST, MOST), MOST)],
            dst_ref=recv_buf.at[pl.ds(pl.multiple_of(slot * MOST, MOST), MOST)],
            send_sem=fs_sem.at[i * NX + dx],
            recv_sem=fr_sem.at[i * NX + dx],
            device_id={"expert": y * NX + x},
            device_id_type=MESH,
        )

    def back_copies(c, half, dx):
        i = c * 2 + half
        y = (my_y - dy_of(c, half) + NY) % NY
        x = (my_x - dx + NX) % NX
        return (
            pltpu.make_async_remote_copy(
                src_ref=back_send.at[pl.ds(pl.multiple_of((i * NX + x) * MOST, MOST), MOST)],
                dst_ref=back_recv.at[pl.ds(pl.multiple_of(me * MOST, MOST), MOST)],
                send_sem=bs_sem.at[i * NX + dx],
                recv_sem=br_sem.at[i * NX + dx],
                device_id={"expert": y * NX + x},
                device_id_type=MESH,
            ),
            pltpu.make_async_remote_copy(
                src_ref=pb_send.at[c],
                dst_ref=pb_recv.at[me],
                send_sem=ps_sem.at[i * NX + dx],
                recv_sem=pr_sem.at[i * NX + dx],
                device_id={"expert": y * NX + x},
                device_id_type=MESH,
            ),
        )

    def each(c, act):
        for half in range(2):
            for dx in range(NX):
                if half == 1 and dx == 0:
                    pl.when(c > 0)(functools.partial(act, half, dx))
                else:
                    act(half, dx)

    pack(0)
    pl.semaphore_wait(barrier, EXPERTS - 1)

    def send(c, carry):
        pl.when(c > 0)(functools.partial(pack, c))
        each(c, lambda half, dx: out_copy(c, half, dx).start())
        return carry

    lax.fori_loop(0, CHUNKS, send, 0)
    own_in = pl.ds(pl.multiple_of((NX + my_x) * MOST, MOST), MOST)
    recv_buf[own_in] = send_buf[own_in]
    for copy in weights:
        copy.wait()

    tile = 256

    def work(c, carry):
        each(c, lambda half, dx: out_copy(c, half, dx).wait_recv())
        at = pl.ds(pl.multiple_of(c * rows, rows), rows)
        x, g = recv_buf[at, :width], recv_buf[at, width:]
        total = jnp.zeros((rows, width), F32)
        prob = jnp.zeros((rows, 1), F32)
        for f in range(0, ff, tile):
            gate_pre = dot(x, wg[:, f : f + tile])
            up_pre = dot(x, wu[:, f : f + tile])
            hidden_grad = dot_t(g, wd[f : f + tile, :])
            sig = jax.nn.sigmoid(gate_pre)
            silu = gate_pre * sig
            prob += jnp.sum(hidden_grad * (silu * up_pre), axis=1, keepdims=True)
            gate_grad = (hidden_grad * up_pre * sig * (1.0 + gate_pre * (1.0 - sig))).astype(BF16)
            up_grad = (hidden_grad * silu).astype(BF16)
            total += dot_t(gate_grad, wg[:, f : f + tile]) + dot_t(up_grad, wu[:, f : f + tile])
        back_send[at] = total.astype(BF16)
        pb_send[c] = jnp.sum(
            jnp.where(eye, prob.astype(BF16).astype(F32), 0.0), axis=0, keepdims=True
        )

        def reply(half, dx):
            for copy in back_copies(c, half, dx):
                copy.start()

        each(c, reply)
        return carry

    lax.fori_loop(0, CHUNKS, work, 0)
    own_back = pl.ds(pl.multiple_of(me * MOST, MOST), MOST)
    back_recv[own_back] = back_send[own_in]
    pb_recv[me] = pb_send[0]

    def finish(c, carry):
        def settle(half, dx):
            out_copy(c, half, dx).wait_send()
            for copy in back_copies(c, half, dx):
                copy.wait()

        each(c, settle)
        return carry

    lax.fori_loop(0, CHUNKS, finish, 0)

    wide = lax.broadcasted_iota(jnp.int32, (tok, EXPERTS * MOST), 1)
    probs = probs_ref[...]
    first = dot((wide == tgt0).astype(BF16), back_recv[...])
    second = dot((wide == tgt1).astype(BF16), back_recv[...])
    out_ref[...] = (first * probs[:, 0:1] + second * probs[:, 1:2]).astype(BF16)

    scores = pb_recv[...].reshape(EXPERTS, tok).astype(BF16)
    expert = lax.broadcasted_iota(jnp.int32, (tok, EXPERTS), 1)
    column = lax.broadcasted_iota(jnp.int32, (tok, TOPK), 1)
    made = []
    for ident, rank in ((id0, rank0), (id1, rank1)):
        mine = dot((expert == ident).astype(BF16), scores)
        dy = (ident // NX - my_y + NY) % NY
        half = jnp.where(jnp.logical_or(dy == 0, dy > 4), 1, 0)
        place = (half * NX + my_x) * MOST + rank
        made.append(jnp.sum(jnp.where(lane == place, mine, 0.0), axis=1, keepdims=True))
    pg_ref[...] = jnp.where(column == 0, made[0], made[1]).astype(BF16)


def per_device(hidden_in, out_grad, gate_probs, expert_ids, w_gate, w_up, w_down):
    tok, width = hidden_in.shape
    ff = w_gate.shape[2]
    slots = EXPERTS * MOST
    vmem = pl.BlockSpec(memory_space=pltpu.VMEM)
    hbm = pl.BlockSpec(memory_space=pl.ANY)
    return pl.pallas_call(
        kernel,
        out_shape=(
            jax.ShapeDtypeStruct((tok, width), BF16),
            jax.ShapeDtypeStruct((tok, TOPK), BF16),
        ),
        in_specs=[vmem, vmem, vmem, vmem, hbm, hbm, hbm],
        out_specs=(vmem, vmem),
        scratch_shapes=[
            pltpu.VMEM((slots, 2 * width), BF16),
            pltpu.VMEM((slots, 2 * width), BF16),
            pltpu.VMEM((slots, width), BF16),
            pltpu.VMEM((slots, width), BF16),
            pltpu.VMEM((CHUNKS, 1, tok), F32),
            pltpu.VMEM((EXPERTS, 1, tok), F32),
            pltpu.VMEM((width, ff), BF16),
            pltpu.VMEM((width, ff), BF16),
            pltpu.VMEM((ff, width), BF16),
            pltpu.SemaphoreType.DMA((3,)),
            pltpu.SemaphoreType.DMA((EXPERTS,)),
            pltpu.SemaphoreType.DMA((EXPERTS,)),
            pltpu.SemaphoreType.DMA((EXPERTS,)),
            pltpu.SemaphoreType.DMA((EXPERTS,)),
            pltpu.SemaphoreType.DMA((EXPERTS,)),
            pltpu.SemaphoreType.DMA((EXPERTS,)),
        ],
        compiler_params=pltpu.CompilerParams(
            collective_id=0, has_side_effects=True, vmem_limit_bytes=48 * 1024 * 1024
        ),
    )(hidden_in, out_grad, gate_probs, expert_ids, w_gate, w_up, w_down)


def solution(mesh):
    in_specs = (
        P(("group", "expert"), None),
        P(("group", "expert"), None),
        P(("group", "expert"), None),
        P(("group", "expert"), None),
        P("expert", None, None),
        P("expert", None, None),
        P("expert", None, None),
    )
    out_specs = (P(("group", "expert"), None), P(("group", "expert"), None))
    return jax.shard_map(
        per_device, mesh=mesh, in_specs=in_specs, out_specs=out_specs, check_vma=False
    )
```

```python
import functools

import jax
import jax.numpy as jnp
from jax import lax
from jax.experimental import pallas as pl
from jax.experimental.pallas import tpu as pltpu
from jax.sharding import PartitionSpec as P

EXPERTS = 32
TOPK = 2
MOST = 16
NX = 4
NY = 8
CHUNKS = 4
PER = EXPERTS // CHUNKS
MESH = pl.DeviceIdType.MESH
BF16 = jnp.bfloat16
F32 = jnp.float32


def dot(a, b):
    return lax.dot_general(a, b, (((1,), (0,)), ((), ())), preferred_element_type=F32)


def dot_t(a, b):
    return lax.dot_general(a, b, (((1,), (1,)), ((), ())), preferred_element_type=F32)


def dy_of(c, half):
    if half == 0:
        return 4 - c
    return jnp.where(c == 0, 0, 4 + c)


def kernel(
    hid_hbm, grad_hbm, probs_hbm, ids_hbm, wg_hbm, wu_hbm, wd_hbm,
    out_ref, pg_ref,
    hid_ref, grad_ref, probs_ref, ids_ref, send_buf, recv_buf, back_send, back_recv, pb_send, pb_recv, wg, wu, wd,
    w_sem, fs_sem, fr_sem, bs_sem, br_sem, ps_sem, pr_sem,
):
    me = lax.axis_index("expert")
    my_y, my_x = me // NX, me % NX
    tok, width = hid_ref.shape
    ff = wg.shape[1]
    rows = PER * MOST

    barrier = pltpu.get_barrier_semaphore()

    def greet(i, carry):
        pl.semaphore_signal(barrier, inc=1, device_id={"expert": (me + i) % EXPERTS}, device_id_type=MESH)
        return carry

    lax.fori_loop(1, EXPERTS, greet, 0)
    ids_in, hid_in, grad_in, probs_in, *weights = (
        pltpu.make_async_copy(ids_hbm, ids_ref, w_sem.at[0]),
        pltpu.make_async_copy(hid_hbm, hid_ref, w_sem.at[1]),
        pltpu.make_async_copy(grad_hbm, grad_ref, w_sem.at[2]),
        pltpu.make_async_copy(probs_hbm, probs_ref, w_sem.at[3]),
        pltpu.make_async_copy(wg_hbm.at[0], wg, w_sem.at[4]),
        pltpu.make_async_copy(wu_hbm.at[0], wu, w_sem.at[5]),
        pltpu.make_async_copy(wd_hbm.at[0], wd, w_sem.at[6]),
    )
    for copy in (ids_in, hid_in, grad_in, probs_in, *weights):
        copy.start()

    ids_in.wait()
    ids = ids_ref[...]
    id0, id1 = ids[0:1, :], ids[1:2, :]
    lane = lax.broadcasted_iota(jnp.int32, (tok, tok), 1)
    sub = lax.broadcasted_iota(jnp.int32, (tok, tok), 0)
    named = jnp.logical_or(sub == id0, sub == id1)
    before = dot(named.astype(BF16), (sub < lane).astype(BF16))
    rank0 = jnp.sum(jnp.where(sub == id0, before, 0.0), axis=0, keepdims=True).astype(jnp.int32)
    rank1 = jnp.sum(jnp.where(sub == id1, before, 0.0), axis=0, keepdims=True).astype(jnp.int32)
    row0, row1 = id0 * MOST + rank0, id1 * MOST + rank1
    eye = lane == sub

    def column(row):
        return jnp.sum(jnp.where(eye, row, jnp.zeros_like(row)), axis=1, keepdims=True)

    def flat(col):
        return jnp.sum(jnp.where(eye, col, jnp.zeros_like(col)), axis=0, keepdims=True)

    half_rows = NX * MOST

    def pack(c):
        s = lax.broadcasted_iota(jnp.int32, (rows, tok), 0)
        y_a, y_b = (my_y + dy_of(c, 0)) % NY, (my_y + dy_of(c, 1)) % NY
        slot = jnp.where(s < half_rows, s + y_a * half_rows, s - half_rows + y_b * half_rows)
        pick = jnp.logical_or(slot == row0, slot == row1).astype(BF16)
        at = pl.ds(pl.multiple_of(c * rows, rows), rows)
        send_buf[at, :width] = dot(pick, hid_ref[...]).astype(BF16)
        send_buf[at, width:] = dot(pick, grad_ref[...]).astype(BF16)

    def out_copy(c, half, dx):
        i = c * 2 + half
        y = (my_y + dy_of(c, half)) % NY
        x = (my_x + dx) % NX
        slot = i * NX + my_x
        return pltpu.make_async_remote_copy(
            src_ref=send_buf.at[pl.ds(pl.multiple_of((i * NX + x) * MOST, MOST), MOST)],
            dst_ref=recv_buf.at[pl.ds(pl.multiple_of(slot * MOST, MOST), MOST)],
            send_sem=fs_sem.at[i * NX + dx],
            recv_sem=fr_sem.at[i * NX + dx],
            device_id={"expert": y * NX + x},
            device_id_type=MESH,
        )

    def back_copies(c, half, dx):
        i = c * 2 + half
        y = (my_y - dy_of(c, half) + NY) % NY
        x = (my_x - dx + NX) % NX
        return (
            pltpu.make_async_remote_copy(
                src_ref=back_send.at[pl.ds(pl.multiple_of((i * NX + x) * MOST, MOST), MOST)],
                dst_ref=back_recv.at[pl.ds(pl.multiple_of(me * MOST, MOST), MOST)],
                send_sem=bs_sem.at[i * NX + dx],
                recv_sem=br_sem.at[i * NX + dx],
                device_id={"expert": y * NX + x},
                device_id_type=MESH,
            ),
            pltpu.make_async_remote_copy(
                src_ref=pb_send.at[c],
                dst_ref=pb_recv.at[me],
                send_sem=ps_sem.at[i * NX + dx],
                recv_sem=pr_sem.at[i * NX + dx],
                device_id={"expert": y * NX + x},
                device_id_type=MESH,
            ),
        )

    def each(c, act):
        for half in range(2):
            for dx in range(NX):
                if half == 1 and dx == 0:
                    pl.when(c > 0)(functools.partial(act, half, dx))
                else:
                    act(half, dx)

    hid_in.wait()
    grad_in.wait()
    pack(0)
    pl.semaphore_wait(barrier, EXPERTS - 1)

    def send(c, carry):
        pl.when(c > 0)(functools.partial(pack, c))
        each(c, lambda half, dx: out_copy(c, half, dx).start())
        return carry

    lax.fori_loop(0, CHUNKS, send, 0)
    own_in = pl.ds(pl.multiple_of((NX + my_x) * MOST, MOST), MOST)
    recv_buf[own_in] = send_buf[own_in]
    for copy in weights:
        copy.wait()

    tile = 256

    def work(c, carry):
        each(c, lambda half, dx: out_copy(c, half, dx).wait_recv())
        at = pl.ds(pl.multiple_of(c * rows, rows), rows)
        x, g = recv_buf[at, :width], recv_buf[at, width:]
        total = jnp.zeros((rows, width), F32)
        prob = jnp.zeros((rows, 1), F32)
        for f in range(0, ff, tile):
            gate_pre = dot(x, wg[:, f : f + tile])
            up_pre = dot(x, wu[:, f : f + tile])
            hidden_grad = dot_t(g, wd[f : f + tile, :])
            sig = jax.nn.sigmoid(gate_pre)
            silu = gate_pre * sig
            prob += jnp.sum(hidden_grad * (silu * up_pre), axis=1, keepdims=True)
            gate_grad = (hidden_grad * up_pre * sig * (1.0 + gate_pre * (1.0 - sig))).astype(BF16)
            up_grad = (hidden_grad * silu).astype(BF16)
            total += dot_t(gate_grad, wg[:, f : f + tile]) + dot_t(up_grad, wu[:, f : f + tile])
        back_send[at] = total.astype(BF16)
        pb_send[c] = flat(prob.astype(BF16).astype(F32))

        def reply(half, dx):
            for copy in back_copies(c, half, dx):
                copy.start()

        each(c, reply)
        return carry

    lax.fori_loop(0, CHUNKS, work, 0)
    own_back = pl.ds(pl.multiple_of(me * MOST, MOST), MOST)
    back_recv[own_back] = back_send[own_in]
    pb_recv[me] = pb_send[0]

    def finish(c, carry):
        def settle(half, dx):
            out_copy(c, half, dx).wait_send()
            for copy in back_copies(c, half, dx):
                copy.wait()

        each(c, settle)
        return carry

    lax.fori_loop(0, CHUNKS, finish, 0)

    wide = lax.broadcasted_iota(jnp.int32, (tok, EXPERTS * MOST), 1)
    probs_in.wait()
    probs = probs_ref[...]
    first = dot((wide == column(row0)).astype(BF16), back_recv[...])
    second = dot((wide == column(row1)).astype(BF16), back_recv[...])
    out_ref[...] = (first * column(probs[0:1, :]) + second * column(probs[1:2, :])).astype(BF16)

    scores = pb_recv[...].reshape(EXPERTS, tok).astype(BF16)
    expert = lax.broadcasted_iota(jnp.int32, (tok, EXPERTS), 1)
    for k, (ident, rank) in enumerate(((id0, rank0), (id1, rank1))):
        mine = dot((expert == column(ident)).astype(BF16), scores)
        dy = (ident // NX - my_y + NY) % NY
        half = jnp.where(jnp.logical_or(dy == 0, dy > 4), 1, 0)
        place = (half * NX + my_x) * MOST + rank
        found = jnp.sum(jnp.where(lane == column(place), mine, 0.0), axis=1, keepdims=True)
        pg_ref[k : k + 1, :] = flat(found).astype(BF16)


def per_device(hidden_in, out_grad, gate_probs, expert_ids, w_gate, w_up, w_down):
    tok, width = hidden_in.shape
    ff = w_gate.shape[2]
    slots = EXPERTS * MOST
    vmem = pl.BlockSpec(memory_space=pltpu.VMEM)
    hbm = pl.BlockSpec(memory_space=pltpu.HBM)
    input_grad, prob_grad = pl.pallas_call(
        kernel,
        out_shape=(
            jax.ShapeDtypeStruct((tok, width), BF16),
            jax.ShapeDtypeStruct((TOPK, tok), BF16),
        ),
        in_specs=[hbm] * 7,
        out_specs=(vmem, vmem),
        scratch_shapes=[
            pltpu.VMEM((tok, width), BF16),
            pltpu.VMEM((tok, width), BF16),
            pltpu.VMEM((TOPK, tok), F32),
            pltpu.VMEM((TOPK, tok), jnp.int32),
            pltpu.VMEM((slots, 2 * width), BF16),
            pltpu.VMEM((slots, 2 * width), BF16),
            pltpu.VMEM((slots, width), BF16),
            pltpu.VMEM((slots, width), BF16),
            pltpu.VMEM((CHUNKS, 1, tok), F32),
            pltpu.VMEM((EXPERTS, 1, tok), F32),
            pltpu.VMEM((width, ff), BF16),
            pltpu.VMEM((width, ff), BF16),
            pltpu.VMEM((ff, width), BF16),
            pltpu.SemaphoreType.DMA((7,)),
            pltpu.SemaphoreType.DMA((EXPERTS,)),
            pltpu.SemaphoreType.DMA((EXPERTS,)),
            pltpu.SemaphoreType.DMA((EXPERTS,)),
            pltpu.SemaphoreType.DMA((EXPERTS,)),
            pltpu.SemaphoreType.DMA((EXPERTS,)),
            pltpu.SemaphoreType.DMA((EXPERTS,)),
        ],
        compiler_params=pltpu.CompilerParams(
            collective_id=0, has_side_effects=True, vmem_limit_bytes=64 * 1024 * 1024
        ),
    )(hidden_in, out_grad, gate_probs.T, expert_ids.T, w_gate, w_up, w_down)
    return input_grad, prob_grad.T


def solution(mesh):
    in_specs = (
        P(("group", "expert"), None),
        P(("group", "expert"), None),
        P(("group", "expert"), None),
        P(("group", "expert"), None),
        P("expert", None, None),
        P("expert", None, None),
        P("expert", None, None),
    )
    out_specs = (P(("group", "expert"), None), P(("group", "expert"), None))
    return jax.shard_map(
        per_device, mesh=mesh, in_specs=in_specs, out_specs=out_specs, check_vma=False
    )
```

```python
import functools

import jax
import jax.numpy as jnp
from jax import lax
from jax.experimental import pallas as pl
from jax.experimental.pallas import tpu as pltpu
from jax.sharding import PartitionSpec as P

EXPERTS = 32
TOPK = 2
MOST = 16
NX = 4
NY = 8
CHUNKS = 4
PER = EXPERTS // CHUNKS
MESH = pl.DeviceIdType.MESH
BF16 = jnp.bfloat16
F32 = jnp.float32


def dot(a, b):
    return lax.dot_general(a, b, (((1,), (0,)), ((), ())), preferred_element_type=F32)


def dot_t(a, b):
    return lax.dot_general(a, b, (((1,), (1,)), ((), ())), preferred_element_type=F32)


def dy_of(c, half):
    if half == 0:
        return 4 - c
    return jnp.where(c == 0, 0, 4 + c)


def kernel(
    hid_hbm, grad_hbm, probs_hbm, ids_hbm, wg_hbm, wu_hbm, wd_hbm,
    out_ref, pg_ref,
    own_tok, probs_ref, ids_ref, near_tok, own_tgt, near_tgt, send_buf, recv_buf,
    back_send, back_recv, pb_send, pb_recv, wg, wu, wd,
    w_sem, ns_sem, nr_sem, fs_sem, fr_sem, bs_sem, br_sem, ps_sem, pr_sem,
):
    me = lax.axis_index("expert")
    my_y, my_x = me // NX, me % NX
    tok, width = hid_hbm.shape
    ff = wg.shape[1]
    rows = PER * MOST
    band = NX * MOST
    reach = NY // 2 * band

    barrier = pltpu.get_barrier_semaphore()

    def greet(i, carry):
        pl.semaphore_signal(barrier, inc=1, device_id={"expert": (me + i) % EXPERTS}, device_id_type=MESH)
        return carry

    ids_in, hid_in, grad_in, probs_in, *weights = (
        pltpu.make_async_copy(ids_hbm, ids_ref, w_sem.at[0]),
        pltpu.make_async_copy(hid_hbm, own_tok.at[0], w_sem.at[1]),
        pltpu.make_async_copy(grad_hbm, own_tok.at[1], w_sem.at[2]),
        pltpu.make_async_copy(probs_hbm, probs_ref, w_sem.at[3]),
        pltpu.make_async_copy(wg_hbm.at[0], wg, w_sem.at[4]),
        pltpu.make_async_copy(wu_hbm.at[0], wu, w_sem.at[5]),
        pltpu.make_async_copy(wd_hbm.at[0], wd, w_sem.at[6]),
    )
    for copy in (ids_in, hid_in, grad_in, probs_in, *weights):
        copy.start()
    lax.fori_loop(1, EXPERTS, greet, 0)

    ids_in.wait()
    ids = ids_ref[...]
    id0, id1 = ids[0:1, :], ids[1:2, :]
    lane = lax.broadcasted_iota(jnp.int32, (tok, tok), 1)
    sub = lax.broadcasted_iota(jnp.int32, (tok, tok), 0)
    named = jnp.logical_or(sub == id0, sub == id1)
    before = dot(named.astype(BF16), (sub < lane).astype(BF16))
    rank0 = jnp.sum(jnp.where(sub == id0, before, 0.0), axis=0, keepdims=True).astype(jnp.int32)
    rank1 = jnp.sum(jnp.where(sub == id1, before, 0.0), axis=0, keepdims=True).astype(jnp.int32)
    row0, row1 = id0 * MOST + rank0, id1 * MOST + rank1
    own_tgt[...] = jnp.where(lax.broadcasted_iota(jnp.int32, own_tgt.shape, 0) == 0, row0, row1)
    eye = lane == sub

    def column(row):
        return jnp.sum(jnp.where(eye, row, jnp.zeros_like(row)), axis=1, keepdims=True)

    def flat(col):
        return jnp.sum(jnp.where(eye, col, jnp.zeros_like(col)), axis=0, keepdims=True)

    def near_copy(side, what):
        src = own_tgt if what == 2 else own_tok.at[what]
        dst = near_tgt.at[side] if what == 2 else near_tok.at[side, what]
        y = (my_y + (1, NY - 1)[side]) % NY
        return pltpu.make_async_remote_copy(
            src_ref=src,
            dst_ref=dst,
            send_sem=ns_sem.at[side, what],
            recv_sem=nr_sem.at[side, what],
            device_id={"expert": y * NX + my_x},
            device_id_type=MESH,
        )

    def pack(tensor, source, tgt, base, first_y, step, count):
        s = lax.broadcasted_iota(jnp.int32, (count, tok), 0)
        slot = ((first_y + step * (s // band) + NY) % NY) * band + s % band
        pick = jnp.logical_or(slot == tgt[0], slot == tgt[1]).astype(BF16)
        send_buf[tensor, base : base + count, :] = dot(pick, source[...]).astype(BF16)

    def out_copy(tensor, c, half, dx):
        own = jnp.logical_and(c == 0, half == 1)
        side = jnp.where(c == 0, dx // 2, half)
        off = jnp.where(own, 0, 3 - c)
        base = jnp.where(own, 2 * reach, side * reach + off * band)
        y = (my_y + (1 - 2 * side) * off + NY) % NY
        x = (my_x + dx) % NX
        i = c * 2 + half
        return pltpu.make_async_remote_copy(
            src_ref=send_buf.at[tensor, pl.ds(pl.multiple_of(base + x * MOST, MOST), MOST)],
            dst_ref=recv_buf.at[tensor, pl.ds(pl.multiple_of((i * NX + my_x) * MOST, MOST), MOST)],
            send_sem=fs_sem.at[tensor, i * NX + dx],
            recv_sem=fr_sem.at[tensor, i * NX + dx],
            device_id={"expert": y * NX + x},
            device_id_type=MESH,
        )

    def each_out(c, act):
        for half in range(2):
            for dx in range(NX):
                if dx > 0:
                    act(half, dx)
                elif half == 0:
                    pl.when(c < 3)(functools.partial(act, half, dx))
                else:
                    pl.when(jnp.logical_and(c > 0, c < 3))(functools.partial(act, half, dx))

    def back_copies(c, half, dx):
        i = c * 2 + half
        y = (my_y - dy_of(c, half) + NY) % NY
        x = (my_x - dx + NX) % NX
        return (
            pltpu.make_async_remote_copy(
                src_ref=back_send.at[pl.ds(pl.multiple_of((i * NX + x) * MOST, MOST), MOST)],
                dst_ref=back_recv.at[pl.ds(pl.multiple_of(me * MOST, MOST), MOST)],
                send_sem=bs_sem.at[i * NX + dx],
                recv_sem=br_sem.at[i * NX + dx],
                device_id={"expert": y * NX + x},
                device_id_type=MESH,
            ),
            pltpu.make_async_remote_copy(
                src_ref=pb_send.at[c],
                dst_ref=pb_recv.at[me],
                send_sem=ps_sem.at[i * NX + dx],
                recv_sem=pr_sem.at[i * NX + dx],
                device_id={"expert": y * NX + x},
                device_id_type=MESH,
            ),
        )

    def each_back(c, act):
        for half in range(2):
            for dx in range(NX):
                if half == 1 and dx == 0:
                    pl.when(c > 0)(functools.partial(act, half, dx))
                else:
                    act(half, dx)

    hid_in.wait()
    grad_in.wait()
    pl.semaphore_wait(barrier, EXPERTS - 1)
    for what in (2, 0, 1):
        for side in range(2):
            near_copy(side, what).start()

    for tensor in range(2):
        pack(tensor, own_tok.at[tensor], (row0, row1), 2 * reach, my_y, 1, band)
    for tensor in range(2):
        for side in range(2):
            if tensor == 0:
                near_copy(side, 2).wait_recv()
            near_copy(side, tensor).wait_recv()
            tgt = near_tgt[side]
            pack(
                tensor, near_tok.at[side, tensor], (tgt[0:1, :], tgt[1:2, :]), side * reach, my_y, 1 - 2 * side, reach
            )

        def send(c, carry):
            each_out(c, lambda half, dx: out_copy(tensor, c, half, dx).start())
            return carry

        lax.fori_loop(0, CHUNKS, send, 0)
        for i, base in ((1, 2 * reach), (6, 0), (7, reach)):
            into = pl.ds(pl.multiple_of((i * NX + my_x) * MOST, MOST), MOST)
            out_of = pl.ds(pl.multiple_of(base + my_x * MOST, MOST), MOST)
            recv_buf[tensor, into] = send_buf[tensor, out_of]
    for copy in weights:
        copy.wait()

    tile = 256

    def work(turn, carry):
        c = (turn + 3) % CHUNKS
        for tensor in range(2):
            each_out(c, lambda half, dx: out_copy(tensor, c, half, dx).wait_recv())
        at = pl.ds(pl.multiple_of(c * rows, rows), rows)
        x, g = recv_buf[0, at], recv_buf[1, at]
        total = jnp.zeros((rows, width), F32)
        prob = jnp.zeros((rows, 1), F32)
        for f in range(0, ff, tile):
            gate_pre = dot(x, wg[:, f : f + tile])
            up_pre = dot(x, wu[:, f : f + tile])
            hidden_grad = dot_t(g, wd[f : f + tile, :])
            sig = jax.nn.sigmoid(gate_pre)
            silu = gate_pre * sig
            prob += jnp.sum(hidden_grad * (silu * up_pre), axis=1, keepdims=True)
            gate_grad = (hidden_grad * up_pre * sig * (1.0 + gate_pre * (1.0 - sig))).astype(BF16)
            up_grad = (hidden_grad * silu).astype(BF16)
            total += dot_t(gate_grad, wg[:, f : f + tile]) + dot_t(up_grad, wu[:, f : f + tile])
        back_send[at] = total.astype(BF16)
        pb_send[c] = flat(prob.astype(BF16).astype(F32))

        def reply(half, dx):
            for copy in back_copies(c, half, dx):
                copy.start()

        each_back(c, reply)
        return carry

    lax.fori_loop(0, CHUNKS, work, 0)
    own_back = pl.ds(pl.multiple_of(me * MOST, MOST), MOST)
    back_recv[own_back] = back_send[pl.ds(pl.multiple_of((NX + my_x) * MOST, MOST), MOST)]
    pb_recv[me] = pb_send[0]

    def finish(c, carry):
        for tensor in range(2):
            each_out(c, lambda half, dx: out_copy(tensor, c, half, dx).wait_send())

        def settle(half, dx):
            for copy in back_copies(c, half, dx):
                copy.wait()

        each_back(c, settle)
        return carry

    lax.fori_loop(0, CHUNKS, finish, 0)
    for what in range(3):
        for side in range(2):
            near_copy(side, what).wait_send()

    wide = lax.broadcasted_iota(jnp.int32, (tok, EXPERTS * MOST), 1)
    probs_in.wait()
    probs = probs_ref[...]
    first = dot((wide == column(row0)).astype(BF16), back_recv[...])
    second = dot((wide == column(row1)).astype(BF16), back_recv[...])
    out_ref[...] = (first * column(probs[0:1, :]) + second * column(probs[1:2, :])).astype(BF16)

    scores = pb_recv[...].reshape(EXPERTS, tok).astype(BF16)
    expert = lax.broadcasted_iota(jnp.int32, (tok, EXPERTS), 1)
    for k, (ident, rank) in enumerate(((id0, rank0), (id1, rank1))):
        mine = dot((expert == column(ident)).astype(BF16), scores)
        dy = (ident // NX - my_y + NY) % NY
        half = jnp.where(jnp.logical_or(dy == 0, dy > 4), 1, 0)
        place = (half * NX + my_x) * MOST + rank
        found = jnp.sum(jnp.where(lane == column(place), mine, 0.0), axis=1, keepdims=True)
        pg_ref[k : k + 1, :] = flat(found).astype(BF16)


def per_device(hidden_in, out_grad, gate_probs, expert_ids, w_gate, w_up, w_down):
    tok, width = hidden_in.shape
    ff = w_gate.shape[2]
    slots = EXPERTS * MOST
    vmem = pl.BlockSpec(memory_space=pltpu.VMEM)
    hbm = pl.BlockSpec(memory_space=pltpu.HBM)
    input_grad, prob_grad = pl.pallas_call(
        kernel,
        out_shape=(
            jax.ShapeDtypeStruct((tok, width), BF16),
            jax.ShapeDtypeStruct((TOPK, tok), BF16),
        ),
        in_specs=[hbm] * 7,
        out_specs=(vmem, vmem),
        scratch_shapes=[
            pltpu.VMEM((2, tok, width), BF16),
            pltpu.VMEM((TOPK, tok), F32),
            pltpu.VMEM((TOPK, tok), jnp.int32),
            pltpu.VMEM((2, 2, tok, width), BF16),
            pltpu.VMEM((8, tok), jnp.int32),
            pltpu.VMEM((2, 8, tok), jnp.int32),
            pltpu.VMEM((2, slots + NX * MOST, width), BF16),
            pltpu.VMEM((2, slots, width), BF16),
            pltpu.VMEM((slots, width), BF16),
            pltpu.VMEM((slots, width), BF16),
            pltpu.VMEM((CHUNKS, 1, tok), F32),
            pltpu.VMEM((EXPERTS, 1, tok), F32),
            pltpu.VMEM((width, ff), BF16),
            pltpu.VMEM((width, ff), BF16),
            pltpu.VMEM((ff, width), BF16),
            pltpu.SemaphoreType.DMA((7,)),
            pltpu.SemaphoreType.DMA((2, 3)),
            pltpu.SemaphoreType.DMA((2, 3)),
            pltpu.SemaphoreType.DMA((2, EXPERTS)),
            pltpu.SemaphoreType.DMA((2, EXPERTS)),
            pltpu.SemaphoreType.DMA((EXPERTS,)),
            pltpu.SemaphoreType.DMA((EXPERTS,)),
            pltpu.SemaphoreType.DMA((EXPERTS,)),
            pltpu.SemaphoreType.DMA((EXPERTS,)),
        ],
        compiler_params=pltpu.CompilerParams(
            collective_id=0, has_side_effects=True, vmem_limit_bytes=64 * 1024 * 1024
        ),
    )(hidden_in, out_grad, gate_probs.T, expert_ids.T, w_gate, w_up, w_down)
    return input_grad, prob_grad.T


def solution(mesh):
    in_specs = (
        P(("group", "expert"), None),
        P(("group", "expert"), None),
        P(("group", "expert"), None),
        P(("group", "expert"), None),
        P("expert", None, None),
        P("expert", None, None),
        P("expert", None, None),
    )
    out_specs = (P(("group", "expert"), None), P(("group", "expert"), None))
    return jax.shard_map(
        per_device, mesh=mesh, in_specs=in_specs, out_specs=out_specs, check_vma=False
    )
```

```python
import functools

import jax
import jax.numpy as jnp
from jax import lax
from jax.experimental import pallas as pl
from jax.experimental.pallas import tpu as pltpu
from jax.sharding import PartitionSpec as P

EXPERTS = 32
TOPK = 2
MOST = 16
NX = 4
NY = 8
CHUNKS = 4
PARTS = 2
PER = EXPERTS // CHUNKS
MESH = pl.DeviceIdType.MESH
BF16 = jnp.bfloat16
F32 = jnp.float32


def dot(a, b):
    return lax.dot_general(a, b, (((1,), (0,)), ((), ())), preferred_element_type=F32)


def dot_t(a, b):
    return lax.dot_general(a, b, (((1,), (1,)), ((), ())), preferred_element_type=F32)


def dy_of(c, half):
    if half == 0:
        return 4 - c
    return jnp.where(c == 0, 0, 4 + c)


def kernel(
    hid_hbm, grad_hbm, probs_hbm, ids_hbm, wg_hbm, wu_hbm, wd_hbm,
    out_ref, pg_ref,
    own_tok, probs_ref, ids_ref, near_tok, own_tgt, near_tgt, own_prob, near_prob, send_buf, recv_buf,
    back_send, back_recv, part_send, part_recv, out_buf, pb_send, pb_recv, wg, wu, wd,
    w_sem, ns_sem, nr_sem, fs_sem, fr_sem, bs_sem, br_sem, ps_sem, pr_sem, ts_sem, tr_sem, o_sem,
):
    me = lax.axis_index("expert")
    my_y, my_x = me // NX, me % NX
    tok, width = hid_hbm.shape
    ff = wg.shape[1]
    rows = PER * MOST
    band = NX * MOST
    reach = NY // 2 * band

    barrier = pltpu.get_barrier_semaphore()

    def greet(i, carry):
        pl.semaphore_signal(barrier, inc=1, device_id={"expert": (me + i) % EXPERTS}, device_id_type=MESH)
        return carry

    ids_in, hid_in, grad_in, probs_in, *weights = (
        pltpu.make_async_copy(ids_hbm, ids_ref, w_sem.at[0]),
        pltpu.make_async_copy(hid_hbm, own_tok.at[0], w_sem.at[1]),
        pltpu.make_async_copy(grad_hbm, own_tok.at[1], w_sem.at[2]),
        pltpu.make_async_copy(probs_hbm, probs_ref, w_sem.at[3]),
        pltpu.make_async_copy(wg_hbm.at[0], wg, w_sem.at[4]),
        pltpu.make_async_copy(wu_hbm.at[0], wu, w_sem.at[5]),
        pltpu.make_async_copy(wd_hbm.at[0], wd, w_sem.at[6]),
    )
    for copy in (ids_in, hid_in, grad_in, probs_in, *weights):
        copy.start()
    lax.fori_loop(1, EXPERTS, greet, 0)

    ids_in.wait()
    ids = ids_ref[...]
    id0, id1 = ids[0:1, :], ids[1:2, :]
    lane = lax.broadcasted_iota(jnp.int32, (tok, tok), 1)
    sub = lax.broadcasted_iota(jnp.int32, (tok, tok), 0)
    named = jnp.logical_or(sub == id0, sub == id1)
    before = dot(named.astype(BF16), (sub < lane).astype(BF16))
    rank0 = jnp.sum(jnp.where(sub == id0, before, 0.0), axis=0, keepdims=True).astype(jnp.int32)
    rank1 = jnp.sum(jnp.where(sub == id1, before, 0.0), axis=0, keepdims=True).astype(jnp.int32)
    row0, row1 = id0 * MOST + rank0, id1 * MOST + rank1
    own_tgt[...] = jnp.where(lax.broadcasted_iota(jnp.int32, own_tgt.shape, 0) == 0, row0, row1)
    eye = lane == sub

    def column(row):
        return jnp.sum(jnp.where(eye, row, jnp.zeros_like(row)), axis=1, keepdims=True)

    def flat(col):
        return jnp.sum(jnp.where(eye, col, jnp.zeros_like(col)), axis=0, keepdims=True)

    def near_copy(side, what):
        src = (own_tok.at[0], own_tok.at[1], own_tgt, own_prob)[what]
        dst = (near_tok.at[side, 0], near_tok.at[side, 1], near_tgt.at[side], near_prob.at[side])[what]
        y = (my_y + (1, NY - 1)[side]) % NY
        return pltpu.make_async_remote_copy(
            src_ref=src,
            dst_ref=dst,
            send_sem=ns_sem.at[side, what],
            recv_sem=nr_sem.at[side, what],
            device_id={"expert": y * NX + my_x},
            device_id_type=MESH,
        )

    def slots_of(shape, axis, step):
        s = lax.broadcasted_iota(jnp.int32, shape, axis)
        return ((my_y + step * (s // band) + NY) % NY) * band + s % band

    def pack(tensor, source, tgt, base, step, count):
        slot = slots_of((count, tok), 0, step)
        pick = jnp.logical_or(slot == tgt[0], slot == tgt[1]).astype(BF16)
        send_buf[tensor, base : base + count, :] = dot(pick, source[...]).astype(BF16)

    def place_of(c, half, dx):
        own = jnp.logical_and(c == 0, half == 1)
        side = jnp.where(c == 0, dx // 2, half)
        off = jnp.where(own, 0, 3 - c)
        return jnp.where(own, 2 * reach, side * reach + off * band), (1 - 2 * side) * off

    def out_copy(tensor, c, half, dx):
        base, off = place_of(c, half, dx)
        y = (my_y + off + NY) % NY
        x = (my_x + dx) % NX
        i = c * 2 + half
        return pltpu.make_async_remote_copy(
            src_ref=send_buf.at[tensor, pl.ds(pl.multiple_of(base + x * MOST, MOST), MOST)],
            dst_ref=recv_buf.at[tensor, pl.ds(pl.multiple_of((i * NX + my_x) * MOST, MOST), MOST)],
            send_sem=fs_sem.at[tensor, i * NX + dx],
            recv_sem=fr_sem.at[tensor, i * NX + dx],
            device_id={"expert": y * NX + x},
            device_id_type=MESH,
        )

    def each_out(c, act):
        for half in range(2):
            for dx in range(NX):
                if dx > 0:
                    act(half, dx)
                elif half == 0:
                    pl.when(c < 3)(functools.partial(act, half, dx))
                else:
                    pl.when(jnp.logical_and(c > 0, c < 3))(functools.partial(act, half, dx))

    def back_copy(c, half, dx):
        base, off = place_of(c, half, dx)
        i = c * 2 + half
        y = (my_y - off + NY) % NY
        x = (my_x - dx + NX) % NX
        return pltpu.make_async_remote_copy(
            src_ref=back_send.at[pl.ds(pl.multiple_of((i * NX + x) * MOST, MOST), MOST)],
            dst_ref=back_recv.at[pl.ds(pl.multiple_of(base + my_x * MOST, MOST), MOST)],
            send_sem=bs_sem.at[i * NX + dx],
            recv_sem=br_sem.at[i * NX + dx],
            device_id={"expert": y * NX + x},
            device_id_type=MESH,
        )

    def prob_copy(c, half, dx):
        i = c * 2 + half
        y = (my_y - dy_of(c, half) + NY) % NY
        x = (my_x - dx + NX) % NX
        return pltpu.make_async_remote_copy(
            src_ref=pb_send.at[c],
            dst_ref=pb_recv.at[me],
            send_sem=ps_sem.at[i * NX + dx],
            recv_sem=pr_sem.at[i * NX + dx],
            device_id={"expert": y * NX + x},
            device_id_type=MESH,
        )

    def part_copy(side, part):
        y = (my_y + (NY - 1, 1)[side]) % NY
        return pltpu.make_async_remote_copy(
            src_ref=part_send.at[side, part],
            dst_ref=part_recv.at[side, part],
            send_sem=ts_sem.at[side, part],
            recv_sem=tr_sem.at[side, part],
            device_id={"expert": y * NX + my_x},
            device_id_type=MESH,
        )

    def each_back(c, act):
        for half in range(2):
            for dx in range(NX):
                if half == 1 and dx == 0:
                    pl.when(c > 0)(functools.partial(act, half, dx))
                else:
                    act(half, dx)

    probs_in.wait()
    probs = probs_ref[...]
    own_prob[...] = jnp.where(
        lax.broadcasted_iota(jnp.int32, own_prob.shape, 0) == 0, probs[0:1, :], probs[1:2, :]
    )
    for side in range(2):
        back_recv[side * reach + 3 * band : (side + 1) * reach, :] = jnp.zeros((band, width), BF16)
    hid_in.wait()
    grad_in.wait()
    pl.semaphore_wait(barrier, EXPERTS - 1)
    for what in (2, 0, 1, 3):
        for side in range(2):
            near_copy(side, what).start()

    for tensor in range(2):
        pack(tensor, own_tok.at[tensor], (row0, row1), 2 * reach, 1, band)
    for tensor in range(2):
        for side in range(2):
            if tensor == 0:
                near_copy(side, 2).wait_recv()
            near_copy(side, tensor).wait_recv()
            tgt = near_tgt[side]
            pack(
                tensor, near_tok.at[side, tensor], (tgt[0:1, :], tgt[1:2, :]), side * reach, 1 - 2 * side, reach
            )

        def send(turn, carry):
            c = CHUNKS - 1 - turn
            each_out(c, lambda half, dx: out_copy(tensor, c, half, dx).start())
            return carry

        lax.fori_loop(0, CHUNKS, send, 0)
        for i, base in ((1, 2 * reach), (6, 0), (7, reach)):
            into = pl.ds(pl.multiple_of((i * NX + my_x) * MOST, MOST), MOST)
            out_of = pl.ds(pl.multiple_of(base + my_x * MOST, MOST), MOST)
            recv_buf[tensor, into] = send_buf[tensor, out_of]
    for copy in weights:
        copy.wait()

    tile = 256

    def work(turn, carry):
        c = CHUNKS - 1 - turn
        for tensor in range(2):
            each_out(c, lambda half, dx: out_copy(tensor, c, half, dx).wait_recv())
        at = pl.ds(pl.multiple_of(c * rows, rows), rows)
        x, g = recv_buf[0, at], recv_buf[1, at]
        total = jnp.zeros((rows, width), F32)
        prob = jnp.zeros((rows, 1), F32)
        for f in range(0, ff, tile):
            gate_pre = dot(x, wg[:, f : f + tile])
            up_pre = dot(x, wu[:, f : f + tile])
            hidden_grad = dot_t(g, wd[f : f + tile, :])
            sig = jax.nn.sigmoid(gate_pre)
            silu = gate_pre * sig
            prob += jnp.sum(hidden_grad * (silu * up_pre), axis=1, keepdims=True)
            gate_grad = (hidden_grad * up_pre * sig * (1.0 + gate_pre * (1.0 - sig))).astype(BF16)
            up_grad = (hidden_grad * silu).astype(BF16)
            total += dot_t(gate_grad, wg[:, f : f + tile]) + dot_t(up_grad, wu[:, f : f + tile])
        back_send[at] = total.astype(BF16)
        pb_send[c] = flat(prob.astype(BF16).astype(F32))

        each_out(c, lambda half, dx: back_copy(c, half, dx).start())
        each_back(c, lambda half, dx: prob_copy(c, half, dx).start())
        return carry

    lax.fori_loop(0, CHUNKS, work, 0)
    for i, base in ((1, 2 * reach), (6, 0), (7, reach)):
        into = pl.ds(pl.multiple_of(base + my_x * MOST, MOST), MOST)
        back_recv[into] = back_send[pl.ds(pl.multiple_of((i * NX + my_x) * MOST, MOST), MOST)]
    pb_recv[me] = pb_send[0]

    parts = part_send.shape[1]
    span = width // parts
    shares = []
    for side in range(2):
        near_copy(side, 3).wait_recv()
        tgt, weight = near_tgt[side], near_prob[side]
        slot = slots_of((tok, reach), 1, 1 - 2 * side)
        shares.append(
            [((slot == column(tgt[k : k + 1, :])).astype(BF16), column(weight[k : k + 1, :])) for k in range(TOPK)]
        )
    slot = slots_of((tok, band), 1, 1)
    own_share = [
        ((slot == column(row)).astype(BF16), column(probs[k : k + 1, :])) for k, row in enumerate((row0, row1))
    ]

    def summed(share, rows_ref):
        (pick_a, weight_a), (pick_b, weight_b) = share
        return dot(pick_a, rows_ref[...]) * weight_a + dot(pick_b, rows_ref[...]) * weight_b

    def arrive(c, carry):
        each_out(c, lambda half, dx: back_copy(c, half, dx).wait_recv())
        return carry

    lax.fori_loop(0, CHUNKS, arrive, 0)
    for part in range(parts):
        cols = slice(part * span, (part + 1) * span)
        for side in range(2):
            rows_ref = back_recv.at[side * reach : (side + 1) * reach, cols]
            part_send[side, part] = summed(shares[side], rows_ref).astype(BF16)
            part_copy(side, part).start()

    def finish(c, carry):
        for tensor in range(2):
            each_out(c, lambda half, dx: out_copy(tensor, c, half, dx).wait_send())
        each_out(c, lambda half, dx: back_copy(c, half, dx).wait_send())
        each_back(c, lambda half, dx: prob_copy(c, half, dx).wait())
        return carry

    lax.fori_loop(0, CHUNKS, finish, 0)
    for what in range(4):
        for side in range(2):
            near_copy(side, what).wait_send()

    scores = pb_recv[...].reshape(EXPERTS, tok).astype(BF16)
    expert = lax.broadcasted_iota(jnp.int32, (tok, EXPERTS), 1)
    for k, (ident, rank) in enumerate(((id0, rank0), (id1, rank1))):
        mine = dot((expert == column(ident)).astype(BF16), scores)
        dy = (ident // NX - my_y + NY) % NY
        half = jnp.where(jnp.logical_or(dy == 0, dy > 4), 1, 0)
        place = (half * NX + my_x) * MOST + rank
        found = jnp.sum(jnp.where(lane == column(place), mine, 0.0), axis=1, keepdims=True)
        pg_ref[k : k + 1, :] = flat(found).astype(BF16)

    results = []
    for part in range(parts):
        cols = slice(part * span, (part + 1) * span)
        own = summed(own_share, back_recv.at[2 * reach : 2 * reach + band, cols])
        for side in range(2):
            part_copy(side, part).wait_recv()
        out_buf[part] = (own + part_recv[0, part].astype(F32) + part_recv[1, part].astype(F32)).astype(BF16)
        results.append(pltpu.make_async_copy(out_buf.at[part], out_ref.at[:, cols], o_sem.at[part]))
        results[-1].start()
    for part in range(parts):
        for side in range(2):
            part_copy(side, part).wait_send()
    for copy in results:
        copy.wait()


def per_device(hidden_in, out_grad, gate_probs, expert_ids, w_gate, w_up, w_down):
    tok, width = hidden_in.shape
    ff = w_gate.shape[2]
    slots = EXPERTS * MOST
    vmem = pl.BlockSpec(memory_space=pltpu.VMEM)
    hbm = pl.BlockSpec(memory_space=pltpu.HBM)
    input_grad, prob_grad = pl.pallas_call(
        kernel,
        out_shape=(
            jax.ShapeDtypeStruct((tok, width), BF16),
            jax.ShapeDtypeStruct((TOPK, tok), BF16),
        ),
        in_specs=[hbm] * 7,
        out_specs=(hbm, vmem),
        scratch_shapes=[
            pltpu.VMEM((2, tok, width), BF16),
            pltpu.VMEM((TOPK, tok), F32),
            pltpu.VMEM((TOPK, tok), jnp.int32),
            pltpu.VMEM((2, 2, tok, width), BF16),
            pltpu.VMEM((8, tok), jnp.int32),
            pltpu.VMEM((2, 8, tok), jnp.int32),
            pltpu.VMEM((8, tok), F32),
            pltpu.VMEM((2, 8, tok), F32),
            pltpu.VMEM((2, slots + NX * MOST, width), BF16),
            pltpu.VMEM((2, slots, width), BF16),
            pltpu.VMEM((slots, width), BF16),
            pltpu.VMEM((slots + NX * MOST, width), BF16),
            pltpu.VMEM((2, PARTS, tok, width // PARTS), BF16),
            pltpu.VMEM((2, PARTS, tok, width // PARTS), BF16),
            pltpu.VMEM((PARTS, tok, width // PARTS), BF16),
            pltpu.VMEM((CHUNKS, 1, tok), F32),
            pltpu.VMEM((EXPERTS, 1, tok), F32),
            pltpu.VMEM((width, ff), BF16),
            pltpu.VMEM((width, ff), BF16),
            pltpu.VMEM((ff, width), BF16),
            pltpu.SemaphoreType.DMA((7,)),
            pltpu.SemaphoreType.DMA((2, 4)),
            pltpu.SemaphoreType.DMA((2, 4)),
            pltpu.SemaphoreType.DMA((2, EXPERTS)),
            pltpu.SemaphoreType.DMA((2, EXPERTS)),
            pltpu.SemaphoreType.DMA((EXPERTS,)),
            pltpu.SemaphoreType.DMA((EXPERTS,)),
            pltpu.SemaphoreType.DMA((EXPERTS,)),
            pltpu.SemaphoreType.DMA((EXPERTS,)),
            pltpu.SemaphoreType.DMA((2, PARTS)),
            pltpu.SemaphoreType.DMA((2, PARTS)),
            pltpu.SemaphoreType.DMA((PARTS,)),
        ],
        compiler_params=pltpu.CompilerParams(
            collective_id=0, has_side_effects=True, vmem_limit_bytes=64 * 1024 * 1024
        ),
    )(hidden_in, out_grad, gate_probs.T, expert_ids.T, w_gate, w_up, w_down)
    return input_grad, prob_grad.T


def solution(mesh):
    in_specs = (
        P(("group", "expert"), None),
        P(("group", "expert"), None),
        P(("group", "expert"), None),
        P(("group", "expert"), None),
        P("expert", None, None),
        P("expert", None, None),
        P("expert", None, None),
    )
    out_specs = (P(("group", "expert"), None), P(("group", "expert"), None))
    return jax.shard_map(
        per_device, mesh=mesh, in_specs=in_specs, out_specs=out_specs, check_vma=False
    )
```

```python
import functools

import jax
import jax.numpy as jnp
from jax import lax
from jax.experimental import pallas as pl
from jax.experimental.pallas import tpu as pltpu
from jax.sharding import PartitionSpec as P

EXPERTS = 32
TOPK = 2
MOST = 16
NX = 4
NY = 8
CHUNKS = 4
ROUNDS = NX // 2 + NY // 2 - 1
PARTS = 2
PER = EXPERTS // CHUNKS
MESH = pl.DeviceIdType.MESH
BF16 = jnp.bfloat16
F32 = jnp.float32


def dot(a, b):
    return lax.dot_general(a, b, (((1,), (0,)), ((), ())), preferred_element_type=F32)


def dot_t(a, b):
    return lax.dot_general(a, b, (((1,), (1,)), ((), ())), preferred_element_type=F32)


def dy_of(c, half):
    if half == 0:
        return 4 - c
    return jnp.where(c == 0, 0, 4 + c)


def kernel(
    hid_hbm, grad_hbm, probs_hbm, ids_hbm, wg_hbm, wu_hbm, wd_hbm,
    out_ref, pg_ref,
    own_tok, probs_ref, ids_ref, near_tok, own_tgt, near_tgt, own_prob, near_prob, send_buf, recv_buf,
    back_send, back_recv, part_send, part_recv, out_buf, pb_send, pb_recv, wg, wu, wd,
    round_sem, w_sem, ns_sem, nr_sem, fs_sem, fr_sem, bs_sem, br_sem, ps_sem, pr_sem, ts_sem, tr_sem, o_sem,
):
    me = lax.axis_index("expert")
    my_y, my_x = me // NX, me % NX
    tok, width = hid_hbm.shape
    ff = wg.shape[1]
    rows = PER * MOST
    band = NX * MOST
    reach = NY // 2 * band

    barrier = pltpu.get_barrier_semaphore()

    neighbours = (
        (my_y + 1) % NY * NX + my_x,
        (my_y + NY - 1) % NY * NX + my_x,
        my_y * NX + (my_x + 1) % NX,
        my_y * NX + (my_x + NX - 1) % NX,
    )

    def greet(sem):
        for other in neighbours:
            pl.semaphore_signal(sem, inc=1, device_id={"expert": other}, device_id_type=MESH)

    ids_in, hid_in, grad_in, probs_in, *weights = (
        pltpu.make_async_copy(ids_hbm, ids_ref, w_sem.at[0]),
        pltpu.make_async_copy(hid_hbm, own_tok.at[0], w_sem.at[1]),
        pltpu.make_async_copy(grad_hbm, own_tok.at[1], w_sem.at[2]),
        pltpu.make_async_copy(probs_hbm, probs_ref, w_sem.at[3]),
        pltpu.make_async_copy(wg_hbm.at[0], wg, w_sem.at[4]),
        pltpu.make_async_copy(wu_hbm.at[0], wu, w_sem.at[5]),
        pltpu.make_async_copy(wd_hbm.at[0], wd, w_sem.at[6]),
    )
    for copy in (ids_in, hid_in, grad_in, probs_in, *weights):
        copy.start()
    greet(barrier)

    ids_in.wait()
    ids = ids_ref[...]
    id0, id1 = ids[0:1, :], ids[1:2, :]
    lane = lax.broadcasted_iota(jnp.int32, (tok, tok), 1)
    sub = lax.broadcasted_iota(jnp.int32, (tok, tok), 0)
    named = jnp.logical_or(sub == id0, sub == id1)
    before = dot(named.astype(BF16), (sub < lane).astype(BF16))
    rank0 = jnp.sum(jnp.where(sub == id0, before, 0.0), axis=0, keepdims=True).astype(jnp.int32)
    rank1 = jnp.sum(jnp.where(sub == id1, before, 0.0), axis=0, keepdims=True).astype(jnp.int32)
    row0, row1 = id0 * MOST + rank0, id1 * MOST + rank1
    own_tgt[...] = jnp.where(lax.broadcasted_iota(jnp.int32, own_tgt.shape, 0) == 0, row0, row1)
    eye = lane == sub

    def column(row):
        return jnp.sum(jnp.where(eye, row, jnp.zeros_like(row)), axis=1, keepdims=True)

    def flat(col):
        return jnp.sum(jnp.where(eye, col, jnp.zeros_like(col)), axis=0, keepdims=True)

    def near_copy(side, what):
        src = (own_tok.at[0], own_tok.at[1], own_tgt, own_prob)[what]
        dst = (near_tok.at[side, 0], near_tok.at[side, 1], near_tgt.at[side], near_prob.at[side])[what]
        y = (my_y + (1, NY - 1)[side]) % NY
        return pltpu.make_async_remote_copy(
            src_ref=src,
            dst_ref=dst,
            send_sem=ns_sem.at[side, what],
            recv_sem=nr_sem.at[side, what],
            device_id={"expert": y * NX + my_x},
            device_id_type=MESH,
        )

    def slots_of(shape, axis, step):
        s = lax.broadcasted_iota(jnp.int32, shape, axis)
        return ((my_y + step * (s // band) + NY) % NY) * band + s % band

    def pack(tensor, source, tgt, base, step, count):
        slot = slots_of((count, tok), 0, step)
        pick = jnp.logical_or(slot == tgt[0], slot == tgt[1]).astype(BF16)
        send_buf[tensor, base : base + count, :] = dot(pick, source[...]).astype(BF16)

    def place_of(c, half, dx):
        own = jnp.logical_and(c == 0, half == 1)
        side = jnp.where(c == 0, dx // 2, half)
        off = jnp.where(own, 0, 3 - c)
        return jnp.where(own, 2 * reach, side * reach + off * band), (1 - 2 * side) * off

    def out_copy(tensor, c, half, dx):
        base, off = place_of(c, half, dx)
        y = (my_y + off + NY) % NY
        x = (my_x + dx) % NX
        i = c * 2 + half
        return pltpu.make_async_remote_copy(
            src_ref=send_buf.at[tensor, pl.ds(pl.multiple_of(base + x * MOST, MOST), MOST)],
            dst_ref=recv_buf.at[tensor, pl.ds(pl.multiple_of((i * NX + my_x) * MOST, MOST), MOST)],
            send_sem=fs_sem.at[tensor, i * NX + dx],
            recv_sem=fr_sem.at[tensor, i * NX + dx],
            device_id={"expert": y * NX + x},
            device_id_type=MESH,
        )

    def each_out(c, act):
        for half in range(2):
            for dx in range(NX):
                if dx > 0:
                    act(half, dx)
                elif half == 0:
                    pl.when(c < 3)(functools.partial(act, half, dx))
                else:
                    pl.when(jnp.logical_and(c > 0, c < 3))(functools.partial(act, half, dx))

    def back_copy(c, half, dx):
        base, off = place_of(c, half, dx)
        i = c * 2 + half
        y = (my_y - off + NY) % NY
        x = (my_x - dx + NX) % NX
        return pltpu.make_async_remote_copy(
            src_ref=back_send.at[pl.ds(pl.multiple_of((i * NX + x) * MOST, MOST), MOST)],
            dst_ref=back_recv.at[pl.ds(pl.multiple_of(base + my_x * MOST, MOST), MOST)],
            send_sem=bs_sem.at[i * NX + dx],
            recv_sem=br_sem.at[i * NX + dx],
            device_id={"expert": y * NX + x},
            device_id_type=MESH,
        )

    def prob_copy(c, half, dx):
        i = c * 2 + half
        y = (my_y - dy_of(c, half) + NY) % NY
        x = (my_x - dx + NX) % NX
        return pltpu.make_async_remote_copy(
            src_ref=pb_send.at[c],
            dst_ref=pb_recv.at[me],
            send_sem=ps_sem.at[i * NX + dx],
            recv_sem=pr_sem.at[i * NX + dx],
            device_id={"expert": y * NX + x},
            device_id_type=MESH,
        )

    def part_copy(side, part):
        y = (my_y + (NY - 1, 1)[side]) % NY
        return pltpu.make_async_remote_copy(
            src_ref=part_send.at[side, part],
            dst_ref=part_recv.at[side, part],
            send_sem=ts_sem.at[side, part],
            recv_sem=tr_sem.at[side, part],
            device_id={"expert": y * NX + my_x},
            device_id_type=MESH,
        )

    def each_back(c, act):
        for half in range(2):
            for dx in range(NX):
                if half == 1 and dx == 0:
                    pl.when(c > 0)(functools.partial(act, half, dx))
                else:
                    act(half, dx)

    probs_in.wait()
    probs = probs_ref[...]
    own_prob[...] = jnp.where(
        lax.broadcasted_iota(jnp.int32, own_prob.shape, 0) == 0, probs[0:1, :], probs[1:2, :]
    )
    for side in range(2):
        back_recv[side * reach + 3 * band : (side + 1) * reach, :] = jnp.zeros((band, width), BF16)
    hid_in.wait()
    grad_in.wait()
    pl.semaphore_wait(barrier, len(neighbours))
    for what in (2, 0, 1, 3):
        for side in range(2):
            near_copy(side, what).start()

    for tensor in range(2):
        pack(tensor, own_tok.at[tensor], (row0, row1), 2 * reach, 1, band)
    for r in range(ROUNDS):
        greet(round_sem.at[r])
        pl.semaphore_wait(round_sem.at[r], len(neighbours))
    for tensor in range(2):
        for side in range(2):
            if tensor == 0:
                near_copy(side, 2).wait_recv()
            near_copy(side, tensor).wait_recv()
            tgt = near_tgt[side]
            pack(
                tensor, near_tok.at[side, tensor], (tgt[0:1, :], tgt[1:2, :]), side * reach, 1 - 2 * side, reach
            )

        def send(turn, carry):
            c = turn
            each_out(c, lambda half, dx: out_copy(tensor, c, half, dx).start())
            return carry

        lax.fori_loop(0, CHUNKS, send, 0)
        for i, base in ((1, 2 * reach), (6, 0), (7, reach)):
            into = pl.ds(pl.multiple_of((i * NX + my_x) * MOST, MOST), MOST)
            out_of = pl.ds(pl.multiple_of(base + my_x * MOST, MOST), MOST)
            recv_buf[tensor, into] = send_buf[tensor, out_of]
    for copy in weights:
        copy.wait()

    tile = 256

    def work(turn, carry):
        c = (turn + 3) % CHUNKS
        for tensor in range(2):
            each_out(c, lambda half, dx: out_copy(tensor, c, half, dx).wait_recv())
        at = pl.ds(pl.multiple_of(c * rows, rows), rows)
        x, g = recv_buf[0, at], recv_buf[1, at]
        total = jnp.zeros((rows, width), F32)
        prob = jnp.zeros((rows, 1), F32)
        for f in range(0, ff, tile):
            gate_pre = dot(x, wg[:, f : f + tile])
            up_pre = dot(x, wu[:, f : f + tile])
            hidden_grad = dot_t(g, wd[f : f + tile, :])
            sig = jax.nn.sigmoid(gate_pre)
            silu = gate_pre * sig
            prob += jnp.sum(hidden_grad * (silu * up_pre), axis=1, keepdims=True)
            gate_grad = (hidden_grad * up_pre * sig * (1.0 + gate_pre * (1.0 - sig))).astype(BF16)
            up_grad = (hidden_grad * silu).astype(BF16)
            total += dot_t(gate_grad, wg[:, f : f + tile]) + dot_t(up_grad, wu[:, f : f + tile])
        back_send[at] = total.astype(BF16)
        pb_send[c] = flat(prob.astype(BF16).astype(F32))

        each_out(c, lambda half, dx: back_copy(c, half, dx).start())
        each_back(c, lambda half, dx: prob_copy(c, half, dx).start())
        return carry

    lax.fori_loop(0, CHUNKS, work, 0)
    for i, base in ((1, 2 * reach), (6, 0), (7, reach)):
        into = pl.ds(pl.multiple_of(base + my_x * MOST, MOST), MOST)
        back_recv[into] = back_send[pl.ds(pl.multiple_of((i * NX + my_x) * MOST, MOST), MOST)]
    pb_recv[me] = pb_send[0]

    parts = part_send.shape[1]
    span = width // parts
    shares = []
    for side in range(2):
        near_copy(side, 3).wait_recv()
        tgt, weight = near_tgt[side], near_prob[side]
        slot = slots_of((tok, reach), 1, 1 - 2 * side)
        shares.append(
            [((slot == column(tgt[k : k + 1, :])).astype(BF16), column(weight[k : k + 1, :])) for k in range(TOPK)]
        )
    slot = slots_of((tok, band), 1, 1)
    own_share = [
        ((slot == column(row)).astype(BF16), column(probs[k : k + 1, :])) for k, row in enumerate((row0, row1))
    ]

    def summed(share, rows_ref):
        (pick_a, weight_a), (pick_b, weight_b) = share
        return dot(pick_a, rows_ref[...]) * weight_a + dot(pick_b, rows_ref[...]) * weight_b

    def arrive(c, carry):
        each_out(c, lambda half, dx: back_copy(c, half, dx).wait_recv())
        return carry

    lax.fori_loop(0, CHUNKS, arrive, 0)
    for part in range(parts):
        cols = slice(part * span, (part + 1) * span)
        for side in range(2):
            rows_ref = back_recv.at[side * reach : (side + 1) * reach, cols]
            part_send[side, part] = summed(shares[side], rows_ref).astype(BF16)
            part_copy(side, part).start()

    def finish(c, carry):
        for tensor in range(2):
            each_out(c, lambda half, dx: out_copy(tensor, c, half, dx).wait_send())
        each_out(c, lambda half, dx: back_copy(c, half, dx).wait_send())
        each_back(c, lambda half, dx: prob_copy(c, half, dx).wait())
        return carry

    lax.fori_loop(0, CHUNKS, finish, 0)
    for what in range(4):
        for side in range(2):
            near_copy(side, what).wait_send()

    scores = pb_recv[...].reshape(EXPERTS, tok).astype(BF16)
    expert = lax.broadcasted_iota(jnp.int32, (tok, EXPERTS), 1)
    for k, (ident, rank) in enumerate(((id0, rank0), (id1, rank1))):
        mine = dot((expert == column(ident)).astype(BF16), scores)
        dy = (ident // NX - my_y + NY) % NY
        half = jnp.where(jnp.logical_or(dy == 0, dy > 4), 1, 0)
        place = (half * NX + my_x) * MOST + rank
        found = jnp.sum(jnp.where(lane == column(place), mine, 0.0), axis=1, keepdims=True)
        pg_ref[k : k + 1, :] = flat(found).astype(BF16)

    results = []
    for part in range(parts):
        cols = slice(part * span, (part + 1) * span)
        own = summed(own_share, back_recv.at[2 * reach : 2 * reach + band, cols])
        for side in range(2):
            part_copy(side, part).wait_recv()
        out_buf[part] = (own + part_recv[0, part].astype(F32) + part_recv[1, part].astype(F32)).astype(BF16)
        results.append(pltpu.make_async_copy(out_buf.at[part], out_ref.at[:, cols], o_sem.at[part]))
        results[-1].start()
    for part in range(parts):
        for side in range(2):
            part_copy(side, part).wait_send()
    for copy in results:
        copy.wait()


def per_device(hidden_in, out_grad, gate_probs, expert_ids, w_gate, w_up, w_down):
    tok, width = hidden_in.shape
    ff = w_gate.shape[2]
    slots = EXPERTS * MOST
    vmem = pl.BlockSpec(memory_space=pltpu.VMEM)
    hbm = pl.BlockSpec(memory_space=pltpu.HBM)
    input_grad, prob_grad = pl.pallas_call(
        kernel,
        out_shape=(
            jax.ShapeDtypeStruct((tok, width), BF16),
            jax.ShapeDtypeStruct((TOPK, tok), BF16),
        ),
        in_specs=[hbm] * 7,
        out_specs=(hbm, vmem),
        scratch_shapes=[
            pltpu.VMEM((2, tok, width), BF16),
            pltpu.VMEM((TOPK, tok), F32),
            pltpu.VMEM((TOPK, tok), jnp.int32),
            pltpu.VMEM((2, 2, tok, width), BF16),
            pltpu.VMEM((8, tok), jnp.int32),
            pltpu.VMEM((2, 8, tok), jnp.int32),
            pltpu.VMEM((8, tok), F32),
            pltpu.VMEM((2, 8, tok), F32),
            pltpu.VMEM((2, slots + NX * MOST, width), BF16),
            pltpu.VMEM((2, slots, width), BF16),
            pltpu.VMEM((slots, width), BF16),
            pltpu.VMEM((slots + NX * MOST, width), BF16),
            pltpu.VMEM((2, PARTS, tok, width // PARTS), BF16),
            pltpu.VMEM((2, PARTS, tok, width // PARTS), BF16),
            pltpu.VMEM((PARTS, tok, width // PARTS), BF16),
            pltpu.VMEM((CHUNKS, 1, tok), F32),
            pltpu.VMEM((EXPERTS, 1, tok), F32),
            pltpu.VMEM((width, ff), BF16),
            pltpu.VMEM((width, ff), BF16),
            pltpu.VMEM((ff, width), BF16),
            pltpu.SemaphoreType.REGULAR((ROUNDS,)),
            pltpu.SemaphoreType.DMA((7,)),
            pltpu.SemaphoreType.DMA((2, 4)),
            pltpu.SemaphoreType.DMA((2, 4)),
            pltpu.SemaphoreType.DMA((2, EXPERTS)),
            pltpu.SemaphoreType.DMA((2, EXPERTS)),
            pltpu.SemaphoreType.DMA((EXPERTS,)),
            pltpu.SemaphoreType.DMA((EXPERTS,)),
            pltpu.SemaphoreType.DMA((EXPERTS,)),
            pltpu.SemaphoreType.DMA((EXPERTS,)),
            pltpu.SemaphoreType.DMA((2, PARTS)),
            pltpu.SemaphoreType.DMA((2, PARTS)),
            pltpu.SemaphoreType.DMA((PARTS,)),
        ],
        compiler_params=pltpu.CompilerParams(
            collective_id=0, has_side_effects=True, vmem_limit_bytes=64 * 1024 * 1024
        ),
    )(hidden_in, out_grad, gate_probs.T, expert_ids.T, w_gate, w_up, w_down)
    return input_grad, prob_grad.T


def solution(mesh):
    in_specs = (
        P(("group", "expert"), None),
        P(("group", "expert"), None),
        P(("group", "expert"), None),
        P(("group", "expert"), None),
        P("expert", None, None),
        P("expert", None, None),
        P("expert", None, None),
    )
    out_specs = (P(("group", "expert"), None), P(("group", "expert"), None))
    return jax.shard_map(
        per_device, mesh=mesh, in_specs=in_specs, out_specs=out_specs, check_vma=False
    )
```

```python
import functools

import jax
import jax.numpy as jnp
from jax import lax
from jax.experimental import pallas as pl
from jax.experimental.pallas import tpu as pltpu
from jax.sharding import PartitionSpec as P

EXPERTS = 32
TOPK = 2
MOST = 16
NX = 4
NY = 8
CHUNKS = 4
ROUNDS = 3
PARTS = 2
PIECES = 2
PER = EXPERTS // CHUNKS
MESH = pl.DeviceIdType.MESH
BF16 = jnp.bfloat16
F32 = jnp.float32


def dot(a, b):
    return lax.dot_general(a, b, (((1,), (0,)), ((), ())), preferred_element_type=F32)


def dot_t(a, b):
    return lax.dot_general(a, b, (((1,), (1,)), ((), ())), preferred_element_type=F32)


def dy_of(c, half):
    if half == 0:
        return 4 - c
    return jnp.where(c == 0, 0, 4 + c)


def kernel(
    hid_hbm, grad_hbm, probs_hbm, ids_hbm, wg_hbm, wu_hbm, wd_hbm,
    out_ref, pg_ref,
    own_tok, probs_ref, ids_ref, near_tok, own_tgt, near_tgt, own_prob, near_prob, send_buf, recv_buf,
    back_send, back_recv, part_send, part_recv, out_buf, pb_send, pb_recv, wg, wu, wd,
    round_sem, w_sem, ns_sem, nr_sem, fs_sem, fr_sem, bs_sem, br_sem, ps_sem, pr_sem, ts_sem, tr_sem, o_sem,
):
    me = lax.axis_index("expert")
    my_y, my_x = me // NX, me % NX
    tok, width = hid_hbm.shape
    ff = wg.shape[1]
    rows = PER * MOST
    band = NX * MOST
    reach = NY // 2 * band

    barrier = pltpu.get_barrier_semaphore()

    neighbours = (
        (my_y + 1) % NY * NX + my_x,
        (my_y + NY - 1) % NY * NX + my_x,
        my_y * NX + (my_x + 1) % NX,
        my_y * NX + (my_x + NX - 1) % NX,
    )

    two_away = (
        (my_y + 2) % NY * NX + my_x,
        (my_y + NY - 2) % NY * NX + my_x,
        my_y * NX + (my_x + 2) % NX,
    )

    def greet(sem, others):
        for other in others:
            pl.semaphore_signal(sem, inc=1, device_id={"expert": other}, device_id_type=MESH)

    ids_in, hid_in, grad_in, probs_in, *weights = (
        pltpu.make_async_copy(ids_hbm, ids_ref, w_sem.at[0]),
        pltpu.make_async_copy(hid_hbm, own_tok.at[0], w_sem.at[1]),
        pltpu.make_async_copy(grad_hbm, own_tok.at[1], w_sem.at[2]),
        pltpu.make_async_copy(probs_hbm, probs_ref, w_sem.at[3]),
        pltpu.make_async_copy(wg_hbm.at[0], wg, w_sem.at[4]),
        pltpu.make_async_copy(wu_hbm.at[0], wu, w_sem.at[5]),
        pltpu.make_async_copy(wd_hbm.at[0], wd, w_sem.at[6]),
    )
    for copy in (ids_in, hid_in, grad_in, probs_in, *weights):
        copy.start()
    greet(barrier, neighbours)

    ids_in.wait()
    ids = ids_ref[...]
    id0, id1 = ids[0:1, :], ids[1:2, :]
    lane = lax.broadcasted_iota(jnp.int32, (tok, tok), 1)
    sub = lax.broadcasted_iota(jnp.int32, (tok, tok), 0)
    named = jnp.logical_or(sub == id0, sub == id1)
    before = dot(named.astype(BF16), (sub < lane).astype(BF16))
    rank0 = jnp.sum(jnp.where(sub == id0, before, 0.0), axis=0, keepdims=True).astype(jnp.int32)
    rank1 = jnp.sum(jnp.where(sub == id1, before, 0.0), axis=0, keepdims=True).astype(jnp.int32)
    row0, row1 = id0 * MOST + rank0, id1 * MOST + rank1
    own_tgt[...] = jnp.where(lax.broadcasted_iota(jnp.int32, own_tgt.shape, 0) == 0, row0, row1)
    eye = lane == sub

    def column(row):
        return jnp.sum(jnp.where(eye, row, jnp.zeros_like(row)), axis=1, keepdims=True)

    def flat(col):
        return jnp.sum(jnp.where(eye, col, jnp.zeros_like(col)), axis=0, keepdims=True)

    def near_copy(side, what):
        src = (own_tok.at[0], own_tok.at[1], own_tgt, own_prob)[what]
        dst = (near_tok.at[side, 0], near_tok.at[side, 1], near_tgt.at[side], near_prob.at[side])[what]
        y = (my_y + (1, NY - 1)[side]) % NY
        return pltpu.make_async_remote_copy(
            src_ref=src,
            dst_ref=dst,
            send_sem=ns_sem.at[side, what],
            recv_sem=nr_sem.at[side, what],
            device_id={"expert": y * NX + my_x},
            device_id_type=MESH,
        )

    def slots_of(shape, axis, step):
        s = lax.broadcasted_iota(jnp.int32, shape, axis)
        return ((my_y + step * (s // band) + NY) % NY) * band + s % band

    def pack(tensor, source, tgt, base, step, count):
        slot = slots_of((count, tok), 0, step)
        pick = jnp.logical_or(slot == tgt[0], slot == tgt[1]).astype(BF16)
        send_buf[tensor, base : base + count, :] = dot(pick, source[...]).astype(BF16)

    def place_of(c, half, dx):
        own = jnp.logical_and(c == 0, half == 1)
        side = jnp.where(c == 0, dx // 2, half)
        off = jnp.where(own, 0, 3 - c)
        return jnp.where(own, 2 * reach, side * reach + off * band), (1 - 2 * side) * off

    def out_copy(tensor, c, half, dx):
        base, off = place_of(c, half, dx)
        y = (my_y + off + NY) % NY
        x = (my_x + dx) % NX
        i = c * 2 + half
        return pltpu.make_async_remote_copy(
            src_ref=send_buf.at[tensor, pl.ds(pl.multiple_of(base + x * MOST, MOST), MOST)],
            dst_ref=recv_buf.at[tensor, pl.ds(pl.multiple_of((i * NX + my_x) * MOST, MOST), MOST)],
            send_sem=fs_sem.at[tensor, i * NX + dx],
            recv_sem=fr_sem.at[tensor, i * NX + dx],
            device_id={"expert": y * NX + x},
            device_id_type=MESH,
        )

    def each_out(c, act):
        for half in range(2):
            for dx in range(NX):
                if dx > 0:
                    act(half, dx)
                elif half == 0:
                    pl.when(c < 3)(functools.partial(act, half, dx))
                else:
                    pl.when(jnp.logical_and(c > 0, c < 3))(functools.partial(act, half, dx))

    def back_copy(c, half, dx):
        base, off = place_of(c, half, dx)
        i = c * 2 + half
        y = (my_y - off + NY) % NY
        x = (my_x - dx + NX) % NX
        return pltpu.make_async_remote_copy(
            src_ref=back_send.at[pl.ds(pl.multiple_of((i * NX + x) * MOST, MOST), MOST)],
            dst_ref=back_recv.at[pl.ds(pl.multiple_of(base + my_x * MOST, MOST), MOST)],
            send_sem=bs_sem.at[i * NX + dx],
            recv_sem=br_sem.at[i * NX + dx],
            device_id={"expert": y * NX + x},
            device_id_type=MESH,
        )

    def prob_copy(c, half, dx):
        i = c * 2 + half
        y = (my_y - dy_of(c, half) + NY) % NY
        x = (my_x - dx + NX) % NX
        return pltpu.make_async_remote_copy(
            src_ref=pb_send.at[c],
            dst_ref=pb_recv.at[me],
            send_sem=ps_sem.at[i * NX + dx],
            recv_sem=pr_sem.at[i * NX + dx],
            device_id={"expert": y * NX + x},
            device_id_type=MESH,
        )

    def part_copy(side, part):
        y = (my_y + (NY - 1, 1)[side]) % NY
        return pltpu.make_async_remote_copy(
            src_ref=part_send.at[side, part],
            dst_ref=part_recv.at[side, part],
            send_sem=ts_sem.at[side, part],
            recv_sem=tr_sem.at[side, part],
            device_id={"expert": y * NX + my_x},
            device_id_type=MESH,
        )

    def each_back(c, act):
        for half in range(2):
            for dx in range(NX):
                if half == 1 and dx == 0:
                    pl.when(c > 0)(functools.partial(act, half, dx))
                else:
                    act(half, dx)

    probs_in.wait()
    probs = probs_ref[...]
    own_prob[...] = jnp.where(
        lax.broadcasted_iota(jnp.int32, own_prob.shape, 0) == 0, probs[0:1, :], probs[1:2, :]
    )
    for side in range(2):
        back_recv[side * reach + 3 * band : (side + 1) * reach, :] = jnp.zeros((band, width), BF16)
    hid_in.wait()
    grad_in.wait()
    pl.semaphore_wait(barrier, len(neighbours))
    for what in (2, 0, 1, 3):
        for side in range(2):
            near_copy(side, what).start()

    for tensor in range(2):
        pack(tensor, own_tok.at[tensor], (row0, row1), 2 * reach, 1, band)
    for r, others in enumerate((neighbours, two_away, two_away)):
        greet(round_sem.at[r], others)
        pl.semaphore_wait(round_sem.at[r], len(others))
    for tensor in range(2):
        for side in range(2):
            if tensor == 0:
                near_copy(side, 2).wait_recv()
            near_copy(side, tensor).wait_recv()
            tgt = near_tgt[side]
            pack(
                tensor, near_tok.at[side, tensor], (tgt[0:1, :], tgt[1:2, :]), side * reach, 1 - 2 * side, reach
            )

        def send(turn, carry):
            c = (turn + 3) % CHUNKS
            each_out(c, lambda half, dx: out_copy(tensor, c, half, dx).start())
            return carry

        lax.fori_loop(0, CHUNKS, send, 0)
        for i, base in ((1, 2 * reach), (6, 0), (7, reach)):
            into = pl.ds(pl.multiple_of((i * NX + my_x) * MOST, MOST), MOST)
            out_of = pl.ds(pl.multiple_of(base + my_x * MOST, MOST), MOST)
            recv_buf[tensor, into] = send_buf[tensor, out_of]
    for copy in weights:
        copy.wait()

    tile = 256

    def work(turn, carry):
        c = (turn + 3) % CHUNKS
        for tensor in range(2):
            each_out(c, lambda half, dx: out_copy(tensor, c, half, dx).wait_recv())
        at = pl.ds(pl.multiple_of(c * rows, rows), rows)
        x, g = recv_buf[0, at], recv_buf[1, at]
        total = jnp.zeros((rows, width), F32)
        prob = jnp.zeros((rows, 1), F32)
        for f in range(0, ff, tile):
            gate_pre = dot(x, wg[:, f : f + tile])
            up_pre = dot(x, wu[:, f : f + tile])
            hidden_grad = dot_t(g, wd[f : f + tile, :])
            sig = jax.nn.sigmoid(gate_pre)
            silu = gate_pre * sig
            prob += jnp.sum(hidden_grad * (silu * up_pre), axis=1, keepdims=True)
            gate_grad = (hidden_grad * up_pre * sig * (1.0 + gate_pre * (1.0 - sig))).astype(BF16)
            up_grad = (hidden_grad * silu).astype(BF16)
            total += dot_t(gate_grad, wg[:, f : f + tile]) + dot_t(up_grad, wu[:, f : f + tile])
        back_send[at] = total.astype(BF16)
        pb_send[c] = flat(prob.astype(BF16).astype(F32))

        each_out(c, lambda half, dx: back_copy(c, half, dx).start())
        each_back(c, lambda half, dx: prob_copy(c, half, dx).start())
        return carry

    lax.fori_loop(0, CHUNKS, work, 0)
    for i, base in ((1, 2 * reach), (6, 0), (7, reach)):
        into = pl.ds(pl.multiple_of(base + my_x * MOST, MOST), MOST)
        back_recv[into] = back_send[pl.ds(pl.multiple_of((i * NX + my_x) * MOST, MOST), MOST)]
    pb_recv[me] = pb_send[0]

    parts = part_send.shape[1]
    span = width // parts
    shares = []
    for side in range(2):
        near_copy(side, 3).wait_recv()
        tgt, weight = near_tgt[side], near_prob[side]
        slot = slots_of((tok, reach), 1, 1 - 2 * side)
        shares.append(
            [((slot == column(tgt[k : k + 1, :])).astype(BF16), column(weight[k : k + 1, :])) for k in range(TOPK)]
        )
    slot = slots_of((tok, band), 1, 1)
    own_share = [
        ((slot == column(row)).astype(BF16), column(probs[k : k + 1, :])) for k, row in enumerate((row0, row1))
    ]

    def summed(share, rows_ref):
        (pick_a, weight_a), (pick_b, weight_b) = share
        return dot(pick_a, rows_ref[...]) * weight_a + dot(pick_b, rows_ref[...]) * weight_b

    def arrive(c, carry):
        each_out(c, lambda half, dx: back_copy(c, half, dx).wait_recv())
        return carry

    lax.fori_loop(0, CHUNKS, arrive, 0)
    for part in range(parts):
        cols = slice(part * span, (part + 1) * span)
        for side in range(2):
            rows_ref = back_recv.at[side * reach : (side + 1) * reach, cols]
            part_send[side, part] = summed(shares[side], rows_ref).astype(BF16)
            part_copy(side, part).start()

    def finish(c, carry):
        for tensor in range(2):
            each_out(c, lambda half, dx: out_copy(tensor, c, half, dx).wait_send())
        each_out(c, lambda half, dx: back_copy(c, half, dx).wait_send())
        each_back(c, lambda half, dx: prob_copy(c, half, dx).wait())
        return carry

    lax.fori_loop(0, CHUNKS, finish, 0)
    for what in range(4):
        for side in range(2):
            near_copy(side, what).wait_send()

    scores = pb_recv[...].reshape(EXPERTS, tok).astype(BF16)
    expert = lax.broadcasted_iota(jnp.int32, (tok, EXPERTS), 1)
    for k, (ident, rank) in enumerate(((id0, rank0), (id1, rank1))):
        mine = dot((expert == column(ident)).astype(BF16), scores)
        dy = (ident // NX - my_y + NY) % NY
        half = jnp.where(jnp.logical_or(dy == 0, dy > 4), 1, 0)
        place = (half * NX + my_x) * MOST + rank
        found = jnp.sum(jnp.where(lane == column(place), mine, 0.0), axis=1, keepdims=True)
        pg_ref[k : k + 1, :] = flat(found).astype(BF16)

    results = []
    for part in range(parts):
        cols = slice(part * span, (part + 1) * span)
        own = summed(own_share, back_recv.at[2 * reach : 2 * reach + band, cols])
        for side in range(2):
            part_copy(side, part).wait_recv()
        out_buf[part] = (own + part_recv[0, part].astype(F32) + part_recv[1, part].astype(F32)).astype(BF16)
        results.append(pltpu.make_async_copy(out_buf.at[part], out_ref.at[:, cols], o_sem.at[part]))
        results[-1].start()
    for part in range(parts):
        for side in range(2):
            part_copy(side, part).wait_send()
    for copy in results:
        copy.wait()


def deliver(grad_in, prob_in, grad_out, prob_out, grad_v, prob_v, in_sem, out_sem):
    step = grad_v.shape[0] // PIECES
    pieces = [(prob_in, prob_v, prob_out)]
    for p in range(PIECES):
        at = pl.ds(p * step, step)
        pieces.append((grad_in.at[at], grad_v.at[at], grad_out.at[at]))
    loads = [pltpu.make_async_copy(src, mid, in_sem.at[p]) for p, (src, mid, dst) in enumerate(pieces)]
    stores = [pltpu.make_async_copy(mid, dst, out_sem.at[p]) for p, (src, mid, dst) in enumerate(pieces)]
    for load in loads:
        load.start()
    for load, store in zip(loads, stores):
        load.wait()
        store.start()
    for store in stores:
        store.wait()


def per_device(hidden_in, out_grad, gate_probs, expert_ids, w_gate, w_up, w_down):
    tok, width = hidden_in.shape
    ff = w_gate.shape[2]
    slots = EXPERTS * MOST
    vmem = pl.BlockSpec(memory_space=pltpu.VMEM)
    hbm = pl.BlockSpec(memory_space=pltpu.HBM)
    input_grad, prob_grad = pl.pallas_call(
        kernel,
        out_shape=(
            jax.ShapeDtypeStruct((tok, width), BF16),
            jax.ShapeDtypeStruct((TOPK, tok), BF16),
        ),
        in_specs=[hbm] * 7,
        out_specs=(hbm, vmem),
        scratch_shapes=[
            pltpu.VMEM((2, tok, width), BF16),
            pltpu.VMEM((TOPK, tok), F32),
            pltpu.VMEM((TOPK, tok), jnp.int32),
            pltpu.VMEM((2, 2, tok, width), BF16),
            pltpu.VMEM((8, tok), jnp.int32),
            pltpu.VMEM((2, 8, tok), jnp.int32),
            pltpu.VMEM((8, tok), F32),
            pltpu.VMEM((2, 8, tok), F32),
            pltpu.VMEM((2, slots + NX * MOST, width), BF16),
            pltpu.VMEM((2, slots, width), BF16),
            pltpu.VMEM((slots, width), BF16),
            pltpu.VMEM((slots + NX * MOST, width), BF16),
            pltpu.VMEM((2, PARTS, tok, width // PARTS), BF16),
            pltpu.VMEM((2, PARTS, tok, width // PARTS), BF16),
            pltpu.VMEM((PARTS, tok, width // PARTS), BF16),
            pltpu.VMEM((CHUNKS, 1, tok), F32),
            pltpu.VMEM((EXPERTS, 1, tok), F32),
            pltpu.VMEM((width, ff), BF16),
            pltpu.VMEM((width, ff), BF16),
            pltpu.VMEM((ff, width), BF16),
            pltpu.SemaphoreType.REGULAR((ROUNDS,)),
            pltpu.SemaphoreType.DMA((7,)),
            pltpu.SemaphoreType.DMA((2, 4)),
            pltpu.SemaphoreType.DMA((2, 4)),
            pltpu.SemaphoreType.DMA((2, EXPERTS)),
            pltpu.SemaphoreType.DMA((2, EXPERTS)),
            pltpu.SemaphoreType.DMA((EXPERTS,)),
            pltpu.SemaphoreType.DMA((EXPERTS,)),
            pltpu.SemaphoreType.DMA((EXPERTS,)),
            pltpu.SemaphoreType.DMA((EXPERTS,)),
            pltpu.SemaphoreType.DMA((2, PARTS)),
            pltpu.SemaphoreType.DMA((2, PARTS)),
            pltpu.SemaphoreType.DMA((PARTS,)),
        ],
        compiler_params=pltpu.CompilerParams(
            collective_id=0, has_side_effects=True, vmem_limit_bytes=64 * 1024 * 1024
        ),
    )(hidden_in, out_grad, gate_probs.T, expert_ids.T, w_gate, w_up, w_down)
    input_grad, prob_grad = pl.pallas_call(
        deliver,
        out_shape=(
            jax.ShapeDtypeStruct((tok, width), BF16),
            jax.ShapeDtypeStruct((TOPK, tok), BF16),
        ),
        in_specs=[hbm] * 2,
        out_specs=(hbm, hbm),
        scratch_shapes=[
            pltpu.VMEM((tok, width), BF16),
            pltpu.VMEM((TOPK, tok), BF16),
            pltpu.SemaphoreType.DMA((PIECES + 1,)),
            pltpu.SemaphoreType.DMA((PIECES + 1,)),
        ],
        compiler_params=pltpu.CompilerParams(vmem_limit_bytes=64 * 1024 * 1024),
    )(input_grad, prob_grad)
    return input_grad, prob_grad.T


def solution(mesh):
    in_specs = (
        P(("group", "expert"), None),
        P(("group", "expert"), None),
        P(("group", "expert"), None),
        P(("group", "expert"), None),
        P("expert", None, None),
        P("expert", None, None),
        P("expert", None, None),
    )
    out_specs = (P(("group", "expert"), None), P(("group", "expert"), None))
    return jax.shard_map(
        per_device, mesh=mesh, in_specs=in_specs, out_specs=out_specs, check_vma=False
    )
```

```python
import functools

import jax
import jax.numpy as jnp
from jax import lax
from jax.experimental import pallas as pl
from jax.experimental.pallas import tpu as pltpu
from jax.sharding import PartitionSpec as P

EXPERTS = 32
TOPK = 2
MOST = 16
NX = 4
NY = 8
CHUNKS = 4
ROUNDS = 3
PARTS = 2
PIECES = 2
PER = EXPERTS // CHUNKS
MESH = pl.DeviceIdType.MESH
BF16 = jnp.bfloat16
F32 = jnp.float32


def dot(a, b):
    return lax.dot_general(a, b, (((1,), (0,)), ((), ())), preferred_element_type=F32)


def dot_t(a, b):
    return lax.dot_general(a, b, (((1,), (1,)), ((), ())), preferred_element_type=F32)


def dy_of(c, half):
    if half == 0:
        return 4 - c
    return jnp.where(c == 0, 0, 4 + c)


def kernel(
    hid_hbm, grad_hbm, probs_hbm, ids_hbm, wg_hbm, wu_hbm, wd_hbm,
    out_ref, pg_ref,
    own_tok, probs_ref, ids_ref, near_tok, own_tgt, near_tgt, own_prob, near_prob, send_buf, recv_buf,
    back_send, back_recv, part_send, part_recv, out_buf, pb_send, pb_recv, wg, wu, wd,
    round_sem, w_sem, ns_sem, nr_sem, fs_sem, fr_sem, bs_sem, br_sem, ps_sem, pr_sem, ts_sem, tr_sem, o_sem,
):
    me = lax.axis_index("expert")
    my_y, my_x = me // NX, me % NX
    tok, width = hid_hbm.shape
    ff = wg.shape[1]
    rows = PER * MOST
    band = NX * MOST
    reach = NY // 2 * band

    barrier = pltpu.get_barrier_semaphore()

    neighbours = (
        (my_y + 1) % NY * NX + my_x,
        (my_y + NY - 1) % NY * NX + my_x,
        my_y * NX + (my_x + 1) % NX,
        my_y * NX + (my_x + NX - 1) % NX,
    )

    two_away = (
        (my_y + 2) % NY * NX + my_x,
        (my_y + NY - 2) % NY * NX + my_x,
        my_y * NX + (my_x + 2) % NX,
    )

    def greet(sem, others):
        for other in others:
            pl.semaphore_signal(sem, inc=1, device_id={"expert": other}, device_id_type=MESH)

    ids_in, hid_in, grad_in, probs_in, *weights = (
        pltpu.make_async_copy(ids_hbm, ids_ref, w_sem.at[0]),
        pltpu.make_async_copy(hid_hbm, own_tok.at[0], w_sem.at[1]),
        pltpu.make_async_copy(grad_hbm, own_tok.at[1], w_sem.at[2]),
        pltpu.make_async_copy(probs_hbm, probs_ref, w_sem.at[3]),
        pltpu.make_async_copy(wg_hbm.at[0], wg, w_sem.at[4]),
        pltpu.make_async_copy(wu_hbm.at[0], wu, w_sem.at[5]),
        pltpu.make_async_copy(wd_hbm.at[0], wd, w_sem.at[6]),
    )
    for copy in (ids_in, hid_in, grad_in, probs_in, *weights):
        copy.start()
    greet(barrier, neighbours)

    ids_in.wait()
    ids = ids_ref[...]
    id0, id1 = ids[0:1, :], ids[1:2, :]
    lane = lax.broadcasted_iota(jnp.int32, (tok, tok), 1)
    sub = lax.broadcasted_iota(jnp.int32, (tok, tok), 0)
    named = jnp.logical_or(sub == id0, sub == id1)
    before = dot(named.astype(BF16), (sub < lane).astype(BF16))
    rank0 = jnp.sum(jnp.where(sub == id0, before, 0.0), axis=0, keepdims=True).astype(jnp.int32)
    rank1 = jnp.sum(jnp.where(sub == id1, before, 0.0), axis=0, keepdims=True).astype(jnp.int32)
    row0, row1 = id0 * MOST + rank0, id1 * MOST + rank1
    own_tgt[...] = jnp.where(lax.broadcasted_iota(jnp.int32, own_tgt.shape, 0) == 0, row0, row1)
    eye = lane == sub

    def column(row):
        return jnp.sum(jnp.where(eye, row, jnp.zeros_like(row)), axis=1, keepdims=True)

    def flat(col):
        return jnp.sum(jnp.where(eye, col, jnp.zeros_like(col)), axis=0, keepdims=True)

    def near_copy(side, what):
        src = (own_tok.at[0], own_tok.at[1], own_tgt, own_prob)[what]
        dst = (near_tok.at[side, 0], near_tok.at[side, 1], near_tgt.at[side], near_prob.at[side])[what]
        y = (my_y + (1, NY - 1)[side]) % NY
        return pltpu.make_async_remote_copy(
            src_ref=src,
            dst_ref=dst,
            send_sem=ns_sem.at[side, what],
            recv_sem=nr_sem.at[side, what],
            device_id={"expert": y * NX + my_x},
            device_id_type=MESH,
        )

    def slots_of(shape, axis, step):
        s = lax.broadcasted_iota(jnp.int32, shape, axis)
        return ((my_y + step * (s // band) + NY) % NY) * band + s % band

    def pack(tensor, source, tgt, base, step, count):
        slot = slots_of((count, tok), 0, step)
        pick = jnp.logical_or(slot == tgt[0], slot == tgt[1]).astype(BF16)
        send_buf[tensor, base : base + count, :] = dot(pick, source[...]).astype(BF16)

    def place_of(c, half, dx):
        own = jnp.logical_and(c == 0, half == 1)
        side = jnp.where(c == 0, dx // 2, half)
        off = jnp.where(own, 0, 3 - c)
        return jnp.where(own, 2 * reach, side * reach + off * band), (1 - 2 * side) * off

    def out_copy(tensor, c, half, dx):
        base, off = place_of(c, half, dx)
        y = (my_y + off + NY) % NY
        x = (my_x + dx) % NX
        i = c * 2 + half
        return pltpu.make_async_remote_copy(
            src_ref=send_buf.at[tensor, pl.ds(pl.multiple_of(base + x * MOST, MOST), MOST)],
            dst_ref=recv_buf.at[tensor, pl.ds(pl.multiple_of((i * NX + my_x) * MOST, MOST), MOST)],
            send_sem=fs_sem.at[tensor, i * NX + dx],
            recv_sem=fr_sem.at[tensor, i * NX + dx],
            device_id={"expert": y * NX + x},
            device_id_type=MESH,
        )

    def each_out(c, act):
        for half in range(2):
            for dx in range(NX):
                if dx > 0:
                    act(half, dx)
                elif half == 0:
                    pl.when(c < 3)(functools.partial(act, half, dx))
                else:
                    pl.when(jnp.logical_and(c > 0, c < 3))(functools.partial(act, half, dx))

    def back_copy(c, half, dx):
        base, off = place_of(c, half, dx)
        i = c * 2 + half
        y = (my_y - off + NY) % NY
        x = (my_x - dx + NX) % NX
        return pltpu.make_async_remote_copy(
            src_ref=back_send.at[pl.ds(pl.multiple_of((i * NX + x) * MOST, MOST), MOST)],
            dst_ref=back_recv.at[pl.ds(pl.multiple_of(base + my_x * MOST, MOST), MOST)],
            send_sem=bs_sem.at[i * NX + dx],
            recv_sem=br_sem.at[i * NX + dx],
            device_id={"expert": y * NX + x},
            device_id_type=MESH,
        )

    def prob_copy(c, half, dx):
        i = c * 2 + half
        y = (my_y - dy_of(c, half) + NY) % NY
        x = (my_x - dx + NX) % NX
        return pltpu.make_async_remote_copy(
            src_ref=pb_send.at[c],
            dst_ref=pb_recv.at[me],
            send_sem=ps_sem.at[i * NX + dx],
            recv_sem=pr_sem.at[i * NX + dx],
            device_id={"expert": y * NX + x},
            device_id_type=MESH,
        )

    def part_copy(side, part):
        y = (my_y + (NY - 1, 1)[side]) % NY
        return pltpu.make_async_remote_copy(
            src_ref=part_send.at[side, part],
            dst_ref=part_recv.at[side, part],
            send_sem=ts_sem.at[side, part],
            recv_sem=tr_sem.at[side, part],
            device_id={"expert": y * NX + my_x},
            device_id_type=MESH,
        )

    def each_back(c, act):
        for half in range(2):
            for dx in range(NX):
                if half == 1 and dx == 0:
                    pl.when(c > 0)(functools.partial(act, half, dx))
                else:
                    act(half, dx)

    probs_in.wait()
    probs = probs_ref[...]
    own_prob[...] = jnp.where(
        lax.broadcasted_iota(jnp.int32, own_prob.shape, 0) == 0, probs[0:1, :], probs[1:2, :]
    )
    for side in range(2):
        back_recv[side * reach + 3 * band : (side + 1) * reach, :] = jnp.zeros((band, width), BF16)
    hid_in.wait()
    grad_in.wait()
    pl.semaphore_wait(barrier, len(neighbours))
    for what in (2, 0, 1, 3):
        for side in range(2):
            near_copy(side, what).start()

    for tensor in range(2):
        pack(tensor, own_tok.at[tensor], (row0, row1), 2 * reach, 1, band)
    for r, others in enumerate((neighbours, two_away, two_away)):
        greet(round_sem.at[r], others)
        pl.semaphore_wait(round_sem.at[r], len(others))
    for tensor in range(2):
        for side in range(2):
            if tensor == 0:
                near_copy(side, 2).wait_recv()
            near_copy(side, tensor).wait_recv()
            tgt = near_tgt[side]
            pack(
                tensor, near_tok.at[side, tensor], (tgt[0:1, :], tgt[1:2, :]), side * reach, 1 - 2 * side, reach
            )

        def send(turn, carry):
            c = turn
            each_out(c, lambda half, dx: out_copy(tensor, c, half, dx).start())
            return carry

        lax.fori_loop(0, CHUNKS, send, 0)
        for i, base in ((1, 2 * reach), (6, 0), (7, reach)):
            into = pl.ds(pl.multiple_of((i * NX + my_x) * MOST, MOST), MOST)
            out_of = pl.ds(pl.multiple_of(base + my_x * MOST, MOST), MOST)
            recv_buf[tensor, into] = send_buf[tensor, out_of]
    for copy in weights:
        copy.wait()

    tile = 256

    def work(turn, carry):
        c = (turn + 3) % CHUNKS
        for tensor in range(2):
            each_out(c, lambda half, dx: out_copy(tensor, c, half, dx).wait_recv())
        at = pl.ds(pl.multiple_of(c * rows, rows), rows)
        x, g = recv_buf[0, at], recv_buf[1, at]
        total = jnp.zeros((rows, width), F32)
        prob = jnp.zeros((rows, 1), F32)
        for f in range(0, ff, tile):
            gate_pre = dot(x, wg[:, f : f + tile])
            up_pre = dot(x, wu[:, f : f + tile])
            hidden_grad = dot_t(g, wd[f : f + tile, :])
            sig = jax.nn.sigmoid(gate_pre)
            silu = gate_pre * sig
            prob += jnp.sum(hidden_grad * (silu * up_pre), axis=1, keepdims=True)
            gate_grad = (hidden_grad * up_pre * sig * (1.0 + gate_pre * (1.0 - sig))).astype(BF16)
            up_grad = (hidden_grad * silu).astype(BF16)
            total += dot_t(gate_grad, wg[:, f : f + tile]) + dot_t(up_grad, wu[:, f : f + tile])
        back_send[at] = total.astype(BF16)
        pb_send[c] = flat(prob.astype(BF16).astype(F32))

        each_out(c, lambda half, dx: back_copy(c, half, dx).start())
        each_back(c, lambda half, dx: prob_copy(c, half, dx).start())
        return carry

    lax.fori_loop(0, CHUNKS, work, 0)
    for i, base in ((1, 2 * reach), (6, 0), (7, reach)):
        into = pl.ds(pl.multiple_of(base + my_x * MOST, MOST), MOST)
        back_recv[into] = back_send[pl.ds(pl.multiple_of((i * NX + my_x) * MOST, MOST), MOST)]
    pb_recv[me] = pb_send[0]

    parts = part_send.shape[1]
    span = width // parts
    shares = []
    for side in range(2):
        near_copy(side, 3).wait_recv()
        tgt, weight = near_tgt[side], near_prob[side]
        slot = slots_of((tok, reach), 1, 1 - 2 * side)
        shares.append(
            [((slot == column(tgt[k : k + 1, :])).astype(BF16), column(weight[k : k + 1, :])) for k in range(TOPK)]
        )
    slot = slots_of((tok, band), 1, 1)
    own_share = [
        ((slot == column(row)).astype(BF16), column(probs[k : k + 1, :])) for k, row in enumerate((row0, row1))
    ]

    def summed(share, rows_ref):
        (pick_a, weight_a), (pick_b, weight_b) = share
        return dot(pick_a, rows_ref[...]) * weight_a + dot(pick_b, rows_ref[...]) * weight_b

    def arrive(c, carry):
        each_out(c, lambda half, dx: back_copy(c, half, dx).wait_recv())
        return carry

    lax.fori_loop(0, CHUNKS, arrive, 0)
    for part in range(parts):
        cols = slice(part * span, (part + 1) * span)
        for side in range(2):
            rows_ref = back_recv.at[side * reach : (side + 1) * reach, cols]
            part_send[side, part] = summed(shares[side], rows_ref).astype(BF16)
            part_copy(side, part).start()

    def finish(c, carry):
        for tensor in range(2):
            each_out(c, lambda half, dx: out_copy(tensor, c, half, dx).wait_send())
        each_out(c, lambda half, dx: back_copy(c, half, dx).wait_send())
        each_back(c, lambda half, dx: prob_copy(c, half, dx).wait())
        return carry

    lax.fori_loop(0, CHUNKS, finish, 0)
    for what in range(4):
        for side in range(2):
            near_copy(side, what).wait_send()

    scores = pb_recv[...].reshape(EXPERTS, tok).astype(BF16)
    expert = lax.broadcasted_iota(jnp.int32, (tok, EXPERTS), 1)
    for k, (ident, rank) in enumerate(((id0, rank0), (id1, rank1))):
        mine = dot((expert == column(ident)).astype(BF16), scores)
        dy = (ident // NX - my_y + NY) % NY
        half = jnp.where(jnp.logical_or(dy == 0, dy > 4), 1, 0)
        place = (half * NX + my_x) * MOST + rank
        found = jnp.sum(jnp.where(lane == column(place), mine, 0.0), axis=1, keepdims=True)
        pg_ref[k : k + 1, :] = flat(found).astype(BF16)

    results = []
    for part in range(parts):
        cols = slice(part * span, (part + 1) * span)
        own = summed(own_share, back_recv.at[2 * reach : 2 * reach + band, cols])
        for side in range(2):
            part_copy(side, part).wait_recv()
        out_buf[part] = (own + part_recv[0, part].astype(F32) + part_recv[1, part].astype(F32)).astype(BF16)
        results.append(pltpu.make_async_copy(out_buf.at[part], out_ref.at[:, cols], o_sem.at[part]))
        results[-1].start()
    for part in range(parts):
        for side in range(2):
            part_copy(side, part).wait_send()
    for copy in results:
        copy.wait()


def deliver(grad_in, prob_in, grad_out, prob_out, grad_v, prob_v, in_sem, out_sem):
    step = grad_v.shape[0] // PIECES
    pieces = [(prob_in, prob_v, prob_out)]
    for p in range(PIECES):
        at = pl.ds(p * step, step)
        pieces.append((grad_in.at[at], grad_v.at[at], grad_out.at[at]))
    loads = [pltpu.make_async_copy(src, mid, in_sem.at[p]) for p, (src, mid, dst) in enumerate(pieces)]
    stores = [pltpu.make_async_copy(mid, dst, out_sem.at[p]) for p, (src, mid, dst) in enumerate(pieces)]
    for load in loads:
        load.start()
    for load, store in zip(loads, stores):
        load.wait()
        store.start()
    for store in stores:
        store.wait()


def per_device(hidden_in, out_grad, gate_probs, expert_ids, w_gate, w_up, w_down):
    tok, width = hidden_in.shape
    ff = w_gate.shape[2]
    slots = EXPERTS * MOST
    vmem = pl.BlockSpec(memory_space=pltpu.VMEM)
    hbm = pl.BlockSpec(memory_space=pltpu.HBM)
    input_grad, prob_grad = pl.pallas_call(
        kernel,
        out_shape=(
            jax.ShapeDtypeStruct((tok, width), BF16),
            jax.ShapeDtypeStruct((TOPK, tok), BF16),
        ),
        in_specs=[hbm] * 7,
        out_specs=(hbm, vmem),
        scratch_shapes=[
            pltpu.VMEM((2, tok, width), BF16),
            pltpu.VMEM((TOPK, tok), F32),
            pltpu.VMEM((TOPK, tok), jnp.int32),
            pltpu.VMEM((2, 2, tok, width), BF16),
            pltpu.VMEM((8, tok), jnp.int32),
            pltpu.VMEM((2, 8, tok), jnp.int32),
            pltpu.VMEM((8, tok), F32),
            pltpu.VMEM((2, 8, tok), F32),
            pltpu.VMEM((2, slots + NX * MOST, width), BF16),
            pltpu.VMEM((2, slots, width), BF16),
            pltpu.VMEM((slots, width), BF16),
            pltpu.VMEM((slots + NX * MOST, width), BF16),
            pltpu.VMEM((2, PARTS, tok, width // PARTS), BF16),
            pltpu.VMEM((2, PARTS, tok, width // PARTS), BF16),
            pltpu.VMEM((PARTS, tok, width // PARTS), BF16),
            pltpu.VMEM((CHUNKS, 1, tok), F32),
            pltpu.VMEM((EXPERTS, 1, tok), F32),
            pltpu.VMEM((width, ff), BF16),
            pltpu.VMEM((width, ff), BF16),
            pltpu.VMEM((ff, width), BF16),
            pltpu.SemaphoreType.REGULAR((ROUNDS,)),
            pltpu.SemaphoreType.DMA((7,)),
            pltpu.SemaphoreType.DMA((2, 4)),
            pltpu.SemaphoreType.DMA((2, 4)),
            pltpu.SemaphoreType.DMA((2, EXPERTS)),
            pltpu.SemaphoreType.DMA((2, EXPERTS)),
            pltpu.SemaphoreType.DMA((EXPERTS,)),
            pltpu.SemaphoreType.DMA((EXPERTS,)),
            pltpu.SemaphoreType.DMA((EXPERTS,)),
            pltpu.SemaphoreType.DMA((EXPERTS,)),
            pltpu.SemaphoreType.DMA((2, PARTS)),
            pltpu.SemaphoreType.DMA((2, PARTS)),
            pltpu.SemaphoreType.DMA((PARTS,)),
        ],
        compiler_params=pltpu.CompilerParams(
            collective_id=0, has_side_effects=True, vmem_limit_bytes=64 * 1024 * 1024
        ),
    )(hidden_in, out_grad, gate_probs.T, expert_ids.T, w_gate, w_up, w_down)
    input_grad, prob_grad = pl.pallas_call(
        deliver,
        out_shape=(
            jax.ShapeDtypeStruct((tok, width), BF16),
            jax.ShapeDtypeStruct((TOPK, tok), BF16),
        ),
        in_specs=[hbm] * 2,
        out_specs=(hbm, hbm),
        scratch_shapes=[
            pltpu.VMEM((tok, width), BF16),
            pltpu.VMEM((TOPK, tok), BF16),
            pltpu.SemaphoreType.DMA((PIECES + 1,)),
            pltpu.SemaphoreType.DMA((PIECES + 1,)),
        ],
        compiler_params=pltpu.CompilerParams(vmem_limit_bytes=64 * 1024 * 1024),
    )(input_grad, prob_grad)
    return input_grad, prob_grad.T


def solution(mesh):
    in_specs = (
        P(("group", "expert"), None),
        P(("group", "expert"), None),
        P(("group", "expert"), None),
        P(("group", "expert"), None),
        P("expert", None, None),
        P("expert", None, None),
        P("expert", None, None),
    )
    out_specs = (P(("group", "expert"), None), P(("group", "expert"), None))
    return jax.shard_map(
        per_device, mesh=mesh, in_specs=in_specs, out_specs=out_specs, check_vma=False
    )
```

```python
import functools

import jax
import jax.numpy as jnp
from jax import lax
from jax.experimental import pallas as pl
from jax.experimental.pallas import tpu as pltpu
from jax.sharding import PartitionSpec as P

EXPERTS = 32
TOPK = 2
MOST = 16
NX = 4
NY = 8
CHUNKS = 4
ROUNDS = 3
PARTS = 2
PIECES = 2
PER = EXPERTS // CHUNKS
MESH = pl.DeviceIdType.MESH
BF16 = jnp.bfloat16
F32 = jnp.float32


def dot(a, b):
    return lax.dot_general(a, b, (((1,), (0,)), ((), ())), preferred_element_type=F32)


def dot_t(a, b):
    return lax.dot_general(a, b, (((1,), (1,)), ((), ())), preferred_element_type=F32)


def dy_of(c, half):
    if half == 0:
        return 4 - c
    return jnp.where(c == 0, 0, 4 + c)


def kernel(
    hid_hbm, grad_hbm, probs_hbm, ids_hbm, wg_hbm, wu_hbm, wd_hbm,
    out_ref, pg_ref,
    own_tok, probs_ref, ids_ref, near_tok, own_tgt, near_tgt, own_prob, near_prob, send_buf, recv_buf,
    back_send, back_recv, part_send, part_recv, out_buf, pb_send, pb_recv, wg, wu, wd,
    round_sem, w_sem, ns_sem, nr_sem, fs_sem, fr_sem, bs_sem, br_sem, ps_sem, pr_sem, ts_sem, tr_sem, o_sem,
):
    me = lax.axis_index("expert")
    my_y, my_x = me // NX, me % NX
    tok, width = hid_hbm.shape
    ff = wg.shape[1]
    rows = PER * MOST
    band = NX * MOST
    reach = NY // 2 * band

    barrier = pltpu.get_barrier_semaphore()

    neighbours = (
        (my_y + 1) % NY * NX + my_x,
        (my_y + NY - 1) % NY * NX + my_x,
        my_y * NX + (my_x + 1) % NX,
        my_y * NX + (my_x + NX - 1) % NX,
    )

    two_away = (
        (my_y + 2) % NY * NX + my_x,
        (my_y + NY - 2) % NY * NX + my_x,
        my_y * NX + (my_x + 2) % NX,
    )

    def greet(sem, others):
        for other in others:
            pl.semaphore_signal(sem, inc=1, device_id={"expert": other}, device_id_type=MESH)

    ids_in, hid_in, grad_in, probs_in, *weights = (
        pltpu.make_async_copy(ids_hbm, ids_ref, w_sem.at[0]),
        pltpu.make_async_copy(hid_hbm, own_tok.at[0], w_sem.at[1]),
        pltpu.make_async_copy(grad_hbm, own_tok.at[1], w_sem.at[2]),
        pltpu.make_async_copy(probs_hbm, probs_ref, w_sem.at[3]),
        pltpu.make_async_copy(wg_hbm.at[0], wg, w_sem.at[4]),
        pltpu.make_async_copy(wu_hbm.at[0], wu, w_sem.at[5]),
        pltpu.make_async_copy(wd_hbm.at[0], wd, w_sem.at[6]),
    )
    for copy in (ids_in, hid_in, grad_in, probs_in, *weights):
        copy.start()
    greet(barrier, neighbours)

    ids_in.wait()
    ids = ids_ref[...]
    id0, id1 = ids[0:1, :], ids[1:2, :]
    lane = lax.broadcasted_iota(jnp.int32, (tok, tok), 1)
    sub = lax.broadcasted_iota(jnp.int32, (tok, tok), 0)
    named = jnp.logical_or(sub == id0, sub == id1)
    before = dot(named.astype(BF16), (sub < lane).astype(BF16))
    rank0 = jnp.sum(jnp.where(sub == id0, before, 0.0), axis=0, keepdims=True).astype(jnp.int32)
    rank1 = jnp.sum(jnp.where(sub == id1, before, 0.0), axis=0, keepdims=True).astype(jnp.int32)
    row0, row1 = id0 * MOST + rank0, id1 * MOST + rank1
    own_tgt[...] = jnp.where(lax.broadcasted_iota(jnp.int32, own_tgt.shape, 0) == 0, row0, row1)
    eye = lane == sub

    def column(row):
        return jnp.sum(jnp.where(eye, row, jnp.zeros_like(row)), axis=1, keepdims=True)

    def flat(col):
        return jnp.sum(jnp.where(eye, col, jnp.zeros_like(col)), axis=0, keepdims=True)

    def near_copy(side, what):
        src = (own_tok.at[0], own_tok.at[1], own_tgt, own_prob)[what]
        dst = (near_tok.at[side, 0], near_tok.at[side, 1], near_tgt.at[side], near_prob.at[side])[what]
        y = (my_y + (1, NY - 1)[side]) % NY
        return pltpu.make_async_remote_copy(
            src_ref=src,
            dst_ref=dst,
            send_sem=ns_sem.at[side, what],
            recv_sem=nr_sem.at[side, what],
            device_id={"expert": y * NX + my_x},
            device_id_type=MESH,
        )

    def slots_of(shape, axis, step):
        s = lax.broadcasted_iota(jnp.int32, shape, axis)
        return ((my_y + step * (s // band) + NY) % NY) * band + s % band

    def pack(tensor, source, tgt, base, step, count):
        slot = slots_of((count, tok), 0, step)
        pick = jnp.logical_or(slot == tgt[0], slot == tgt[1]).astype(BF16)
        send_buf[tensor, base : base + count, :] = dot(pick, source[...]).astype(BF16)

    def place_of(c, half, dx):
        own = jnp.logical_and(c == 0, half == 1)
        side = jnp.where(c == 0, dx // 2, half)
        off = jnp.where(own, 0, 3 - c)
        return jnp.where(own, 2 * reach, side * reach + off * band), (1 - 2 * side) * off

    def out_copy(tensor, c, half, dx):
        base, off = place_of(c, half, dx)
        y = (my_y + off + NY) % NY
        x = (my_x + dx) % NX
        i = c * 2 + half
        return pltpu.make_async_remote_copy(
            src_ref=send_buf.at[tensor, pl.ds(pl.multiple_of(base + x * MOST, MOST), MOST)],
            dst_ref=recv_buf.at[tensor, pl.ds(pl.multiple_of((i * NX + my_x) * MOST, MOST), MOST)],
            send_sem=fs_sem.at[tensor, i * NX + dx],
            recv_sem=fr_sem.at[tensor, i * NX + dx],
            device_id={"expert": y * NX + x},
            device_id_type=MESH,
        )

    def each_out(c, act):
        for half in range(2):
            for dx in range(NX):
                if dx > 0:
                    act(half, dx)
                elif half == 0:
                    pl.when(c < 3)(functools.partial(act, half, dx))
                else:
                    pl.when(jnp.logical_and(c > 0, c < 3))(functools.partial(act, half, dx))

    def back_copy(c, half, dx):
        base, off = place_of(c, half, dx)
        i = c * 2 + half
        y = (my_y - off + NY) % NY
        x = (my_x - dx + NX) % NX
        return pltpu.make_async_remote_copy(
            src_ref=back_send.at[pl.ds(pl.multiple_of((i * NX + x) * MOST, MOST), MOST)],
            dst_ref=back_recv.at[pl.ds(pl.multiple_of(base + my_x * MOST, MOST), MOST)],
            send_sem=bs_sem.at[i * NX + dx],
            recv_sem=br_sem.at[i * NX + dx],
            device_id={"expert": y * NX + x},
            device_id_type=MESH,
        )

    def prob_copy(c, half, dx):
        i = c * 2 + half
        y = (my_y - dy_of(c, half) + NY) % NY
        x = (my_x - dx + NX) % NX
        return pltpu.make_async_remote_copy(
            src_ref=pb_send.at[c],
            dst_ref=pb_recv.at[me],
            send_sem=ps_sem.at[i * NX + dx],
            recv_sem=pr_sem.at[i * NX + dx],
            device_id={"expert": y * NX + x},
            device_id_type=MESH,
        )

    def part_copy(side, part):
        y = (my_y + (NY - 1, 1)[side]) % NY
        return pltpu.make_async_remote_copy(
            src_ref=part_send.at[side, part],
            dst_ref=part_recv.at[side, part],
            send_sem=ts_sem.at[side, part],
            recv_sem=tr_sem.at[side, part],
            device_id={"expert": y * NX + my_x},
            device_id_type=MESH,
        )

    def each_back(c, act):
        for half in range(2):
            for dx in range(NX):
                if half == 1 and dx == 0:
                    pl.when(c > 0)(functools.partial(act, half, dx))
                else:
                    act(half, dx)

    probs_in.wait()
    probs = probs_ref[...]
    own_prob[...] = jnp.where(
        lax.broadcasted_iota(jnp.int32, own_prob.shape, 0) == 0, probs[0:1, :], probs[1:2, :]
    )
    for side in range(2):
        back_recv[side * reach + 3 * band : (side + 1) * reach, :] = jnp.zeros((band, width), BF16)
    hid_in.wait()
    grad_in.wait()
    pl.semaphore_wait(barrier, len(neighbours))
    for what in (2, 0, 1, 3):
        for side in range(2):
            near_copy(side, what).start()

    for r, others in enumerate((neighbours, two_away, two_away)):
        greet(round_sem.at[r], others)
        pl.semaphore_wait(round_sem.at[r], len(others))
    for tensor in range(2):
        pack(tensor, own_tok.at[tensor], (row0, row1), 2 * reach, 1, band)
    for tensor in range(2):
        for side in range(2):
            if tensor == 0:
                near_copy(side, 2).wait_recv()
            near_copy(side, tensor).wait_recv()
            tgt = near_tgt[side]
            pack(
                tensor, near_tok.at[side, tensor], (tgt[0:1, :], tgt[1:2, :]), side * reach, 1 - 2 * side, reach
            )

        def send(turn, carry):
            c = turn
            each_out(c, lambda half, dx: out_copy(tensor, c, half, dx).start())
            return carry

        lax.fori_loop(0, CHUNKS, send, 0)
        for i, base in ((1, 2 * reach), (6, 0), (7, reach)):
            into = pl.ds(pl.multiple_of((i * NX + my_x) * MOST, MOST), MOST)
            out_of = pl.ds(pl.multiple_of(base + my_x * MOST, MOST), MOST)
            recv_buf[tensor, into] = send_buf[tensor, out_of]
    for copy in weights:
        copy.wait()

    tile = 256

    def work(turn, carry):
        c = (turn + 3) % CHUNKS
        for tensor in range(2):
            each_out(c, lambda half, dx: out_copy(tensor, c, half, dx).wait_recv())
        at = pl.ds(pl.multiple_of(c * rows, rows), rows)
        x, g = recv_buf[0, at], recv_buf[1, at]
        total = jnp.zeros((rows, width), F32)
        prob = jnp.zeros((rows, 1), F32)
        for f in range(0, ff, tile):
            gate_pre = dot(x, wg[:, f : f + tile])
            up_pre = dot(x, wu[:, f : f + tile])
            hidden_grad = dot_t(g, wd[f : f + tile, :])
            sig = jax.nn.sigmoid(gate_pre)
            silu = gate_pre * sig
            prob += jnp.sum(hidden_grad * (silu * up_pre), axis=1, keepdims=True)
            gate_grad = (hidden_grad * up_pre * sig * (1.0 + gate_pre * (1.0 - sig))).astype(BF16)
            up_grad = (hidden_grad * silu).astype(BF16)
            total += dot_t(gate_grad, wg[:, f : f + tile]) + dot_t(up_grad, wu[:, f : f + tile])
        back_send[at] = total.astype(BF16)
        pb_send[c] = flat(prob.astype(BF16).astype(F32))

        each_out(c, lambda half, dx: back_copy(c, half, dx).start())
        each_back(c, lambda half, dx: prob_copy(c, half, dx).start())
        return carry

    lax.fori_loop(0, CHUNKS, work, 0)
    for i, base in ((1, 2 * reach), (6, 0), (7, reach)):
        into = pl.ds(pl.multiple_of(base + my_x * MOST, MOST), MOST)
        back_recv[into] = back_send[pl.ds(pl.multiple_of((i * NX + my_x) * MOST, MOST), MOST)]
    pb_recv[me] = pb_send[0]

    parts = part_send.shape[1]
    span = width // parts
    shares = []
    for side in range(2):
        near_copy(side, 3).wait_recv()
        tgt, weight = near_tgt[side], near_prob[side]
        slot = slots_of((tok, reach), 1, 1 - 2 * side)
        shares.append(
            [((slot == column(tgt[k : k + 1, :])).astype(BF16), column(weight[k : k + 1, :])) for k in range(TOPK)]
        )
    slot = slots_of((tok, band), 1, 1)
    own_share = [
        ((slot == column(row)).astype(BF16), column(probs[k : k + 1, :])) for k, row in enumerate((row0, row1))
    ]

    def summed(share, rows_ref):
        (pick_a, weight_a), (pick_b, weight_b) = share
        return dot(pick_a, rows_ref[...]) * weight_a + dot(pick_b, rows_ref[...]) * weight_b

    def arrive(c, carry):
        each_out(c, lambda half, dx: back_copy(c, half, dx).wait_recv())
        return carry

    lax.fori_loop(0, CHUNKS, arrive, 0)
    for part in range(parts):
        cols = slice(part * span, (part + 1) * span)
        for side in range(2):
            rows_ref = back_recv.at[side * reach : (side + 1) * reach, cols]
            part_send[side, part] = summed(shares[side], rows_ref).astype(BF16)
            part_copy(side, part).start()

    def finish(c, carry):
        for tensor in range(2):
            each_out(c, lambda half, dx: out_copy(tensor, c, half, dx).wait_send())
        each_out(c, lambda half, dx: back_copy(c, half, dx).wait_send())
        each_back(c, lambda half, dx: prob_copy(c, half, dx).wait())
        return carry

    lax.fori_loop(0, CHUNKS, finish, 0)
    for what in range(4):
        for side in range(2):
            near_copy(side, what).wait_send()

    scores = pb_recv[...].reshape(EXPERTS, tok).astype(BF16)
    expert = lax.broadcasted_iota(jnp.int32, (tok, EXPERTS), 1)
    for k, (ident, rank) in enumerate(((id0, rank0), (id1, rank1))):
        mine = dot((expert == column(ident)).astype(BF16), scores)
        dy = (ident // NX - my_y + NY) % NY
        half = jnp.where(jnp.logical_or(dy == 0, dy > 4), 1, 0)
        place = (half * NX + my_x) * MOST + rank
        found = jnp.sum(jnp.where(lane == column(place), mine, 0.0), axis=1, keepdims=True)
        pg_ref[k : k + 1, :] = flat(found).astype(BF16)

    results = []
    for part in range(parts):
        cols = slice(part * span, (part + 1) * span)
        own = summed(own_share, back_recv.at[2 * reach : 2 * reach + band, cols])
        for side in range(2):
            part_copy(side, part).wait_recv()
        out_buf[part] = (own + part_recv[0, part].astype(F32) + part_recv[1, part].astype(F32)).astype(BF16)
        results.append(pltpu.make_async_copy(out_buf.at[part], out_ref.at[:, cols], o_sem.at[part]))
        results[-1].start()
    for part in range(parts):
        for side in range(2):
            part_copy(side, part).wait_send()
    for copy in results:
        copy.wait()


def deliver(grad_in, prob_in, grad_out, prob_out, grad_v, prob_v, in_sem, out_sem):
    step = grad_v.shape[0] // PIECES
    pieces = [(prob_in, prob_v, prob_out)]
    for p in range(PIECES):
        at = pl.ds(p * step, step)
        pieces.append((grad_in.at[at], grad_v.at[at], grad_out.at[at]))
    loads = [pltpu.make_async_copy(src, mid, in_sem.at[p]) for p, (src, mid, dst) in enumerate(pieces)]
    stores = [pltpu.make_async_copy(mid, dst, out_sem.at[p]) for p, (src, mid, dst) in enumerate(pieces)]
    for load in loads:
        load.start()
    for load, store in zip(loads, stores):
        load.wait()
        store.start()
    for store in stores:
        store.wait()


def per_device(hidden_in, out_grad, gate_probs, expert_ids, w_gate, w_up, w_down):
    tok, width = hidden_in.shape
    ff = w_gate.shape[2]
    slots = EXPERTS * MOST
    vmem = pl.BlockSpec(memory_space=pltpu.VMEM)
    hbm = pl.BlockSpec(memory_space=pltpu.HBM)
    input_grad, prob_grad = pl.pallas_call(
        kernel,
        out_shape=(
            jax.ShapeDtypeStruct((tok, width), BF16),
            jax.ShapeDtypeStruct((TOPK, tok), BF16),
        ),
        in_specs=[hbm] * 7,
        out_specs=(hbm, vmem),
        scratch_shapes=[
            pltpu.VMEM((2, tok, width), BF16),
            pltpu.VMEM((TOPK, tok), F32),
            pltpu.VMEM((TOPK, tok), jnp.int32),
            pltpu.VMEM((2, 2, tok, width), BF16),
            pltpu.VMEM((8, tok), jnp.int32),
            pltpu.VMEM((2, 8, tok), jnp.int32),
            pltpu.VMEM((8, tok), F32),
            pltpu.VMEM((2, 8, tok), F32),
            pltpu.VMEM((2, slots + NX * MOST, width), BF16),
            pltpu.VMEM((2, slots, width), BF16),
            pltpu.VMEM((slots, width), BF16),
            pltpu.VMEM((slots + NX * MOST, width), BF16),
            pltpu.VMEM((2, PARTS, tok, width // PARTS), BF16),
            pltpu.VMEM((2, PARTS, tok, width // PARTS), BF16),
            pltpu.VMEM((PARTS, tok, width // PARTS), BF16),
            pltpu.VMEM((CHUNKS, 1, tok), F32),
            pltpu.VMEM((EXPERTS, 1, tok), F32),
            pltpu.VMEM((width, ff), BF16),
            pltpu.VMEM((width, ff), BF16),
            pltpu.VMEM((ff, width), BF16),
            pltpu.SemaphoreType.REGULAR((ROUNDS,)),
            pltpu.SemaphoreType.DMA((7,)),
            pltpu.SemaphoreType.DMA((2, 4)),
            pltpu.SemaphoreType.DMA((2, 4)),
            pltpu.SemaphoreType.DMA((2, EXPERTS)),
            pltpu.SemaphoreType.DMA((2, EXPERTS)),
            pltpu.SemaphoreType.DMA((EXPERTS,)),
            pltpu.SemaphoreType.DMA((EXPERTS,)),
            pltpu.SemaphoreType.DMA((EXPERTS,)),
            pltpu.SemaphoreType.DMA((EXPERTS,)),
            pltpu.SemaphoreType.DMA((2, PARTS)),
            pltpu.SemaphoreType.DMA((2, PARTS)),
            pltpu.SemaphoreType.DMA((PARTS,)),
        ],
        compiler_params=pltpu.CompilerParams(
            collective_id=0, has_side_effects=True, vmem_limit_bytes=64 * 1024 * 1024
        ),
    )(hidden_in, out_grad, gate_probs.T, expert_ids.T, w_gate, w_up, w_down)
    input_grad, prob_grad = pl.pallas_call(
        deliver,
        out_shape=(
            jax.ShapeDtypeStruct((tok, width), BF16),
            jax.ShapeDtypeStruct((TOPK, tok), BF16),
        ),
        in_specs=[hbm] * 2,
        out_specs=(hbm, hbm),
        scratch_shapes=[
            pltpu.VMEM((tok, width), BF16),
            pltpu.VMEM((TOPK, tok), BF16),
            pltpu.SemaphoreType.DMA((PIECES + 1,)),
            pltpu.SemaphoreType.DMA((PIECES + 1,)),
        ],
        compiler_params=pltpu.CompilerParams(vmem_limit_bytes=64 * 1024 * 1024),
    )(input_grad, prob_grad)
    return input_grad, prob_grad.T


def solution(mesh):
    in_specs = (
        P(("group", "expert"), None),
        P(("group", "expert"), None),
        P(("group", "expert"), None),
        P(("group", "expert"), None),
        P("expert", None, None),
        P("expert", None, None),
        P("expert", None, None),
    )
    out_specs = (P(("group", "expert"), None), P(("group", "expert"), None))
    return jax.shard_map(
        per_device, mesh=mesh, in_specs=in_specs, out_specs=out_specs, check_vma=False
    )
```
